512 devices in a mesh: batch: 128 (over z, y, core), grp: 4 (over x).
Axes of the slice: x: 4, y: 4, z: 16, core: 2. Of those that a mesh axis runs over, the one named last changes fastest.
Arguments:
- queries: bfloat16 [65536, 4096], P(('batch', 'grp')), may hold values from -16 to 16
- passages: bfloat16 [65536, 4096], P(('batch', 'grp')), may hold values from -16 to 16
- hard_ids: int32 [65536], P(('batch', 'grp')), may hold values from 0 to 16383, as said below
Outputs:
- query_grad: bfloat16 [65536, 4096], P(('batch', 'grp'))
- passage_grad: bfloat16 [65536, 4096], P(('batch', 'grp'))
The draws below stay inside these ranges and needn't reach their ends.
Inputs may be any that keep to these rules, and one draw needn't show every extreme that they name: `hard_ids`: an entry v names the passage at offset v % 128 of the device with batch index v // 128 and the query's grp index; the queries of one device name at most 2 rows held by any one device, exactly 2 on some device, and in every grp index some device is named 2 times by every device of that grp index.
All inputs are finite; a program needn't handle non-finite values.
Results may differ from the reference program's by a relative error of at most 0.0095.
Values may be sent and summed in bfloat16 or wider, within the bound.
A program may use at most 64 MiB of HBM per device.

```python
import jax
import jax.numpy as jnp
from jax import lax

EMBED_DIMENSION = 4096
PAIRS_DEV = 128
CAP = 2
GROUP = 512
PAIRS = 65536
BLOCKS = 512
N_BATCH = 128
N_GRP = 4


def hard_choice(key):
    key = jax.random.fold_in(key, 21)
    keys = jax.random.split(key, 6)
    span = N_BATCH * CAP
    favour = jax.random.randint(keys[0], (N_GRP, N_BATCH), 0, 3)
    marked = jax.random.randint(keys[1], (N_GRP,), 0, N_BATCH)
    favour = jnp.where(jnp.arange(N_BATCH)[None, :] == marked[:, None], 3, favour)
    forced = jax.random.randint(keys[2], (BLOCKS,), 0, N_BATCH)
    jitter = jax.random.randint(keys[3], (BLOCKS, span), 0, span)
    entry = jnp.arange(span)
    entry_owner = entry // CAP
    column = jnp.arange(BLOCKS) % N_GRP
    level = favour[column][:, entry_owner] + 8 * (entry_owner[None, :] == forced[:, None]).astype(jnp.int32)
    score = (level * span + jitter) * span + entry[None, :]
    picked = lax.top_k(score, PAIRS_DEV)[1]
    owners = picked // CAP
    order_keys = jax.random.randint(keys[4], (BLOCKS, PAIRS_DEV), 0, PAIRS_DEV) * PAIRS_DEV + jnp.arange(PAIRS_DEV)[None, :]
    order = jnp.argsort(order_keys, axis=1)
    owners = jnp.take_along_axis(owners, order, 1)
    offsets = jax.random.randint(keys[5], (BLOCKS, PAIRS_DEV), 0, PAIRS_DEV)
    return (owners * PAIRS_DEV + offsets).reshape(PAIRS).astype(jnp.int32)


def shared_parts(key):
    first, second, third = jax.random.split(key, 3)
    common = jax.random.normal(first, (PAIRS, EMBED_DIMENSION), jnp.float32)
    direction = jax.random.normal(second, (EMBED_DIMENSION,), jnp.float32)
    loading = jax.random.normal(third, (PAIRS, 1), jnp.float32)
    return (common, direction, loading)


def aligned_rows(key, common):
    ids = hard_choice(key)
    row_index = jnp.arange(PAIRS)
    grp_of = row_index // PAIRS_DEV % N_GRP
    target_labels = (ids // PAIRS_DEV * N_GRP + grp_of) * PAIRS_DEV + ids % PAIRS_DEV
    source = jnp.full((PAIRS,), -1, jnp.int32).at[target_labels].max(row_index.astype(jnp.int32))
    named = (source >= 0).astype(jnp.float32)
    return jnp.take(common, jnp.maximum(source, 0), axis=0) * named[:, None]


def draw_queries(key, part):
    common, direction, loading = shared_parts(key)
    values = common + 0.3 * loading * direction[None, :]
    return jnp.clip(values, -16.0, 16.0).astype(jnp.bfloat16)


def draw_passages(key, part):
    common, direction, loading = shared_parts(key)
    aligned = aligned_rows(key, common)
    key = jax.random.fold_in(key, 12)
    first, second = jax.random.split(key, 2)
    other_load = jax.random.normal(second, (PAIRS, 1), jnp.float32)
    extra = jax.random.normal(first, (PAIRS, EMBED_DIMENSION), jnp.float32)
    values = 0.3 * common + 0.35 * aligned + 0.95 * extra + 0.3 * other_load * direction[None, :]
    return jnp.clip(values, -16.0, 16.0).astype(jnp.bfloat16)


def draw_hard_ids(key, part):
    return hard_choice(key)


def setup_inputs(seed: int = 0) -> dict:
    key_list = jax.random.split(jax.random.key(seed), 4)
    return {
        "queries": draw_queries(jax.random.fold_in(key_list[3], 71), 0),
        "passages": draw_passages(jax.random.fold_in(key_list[3], 71), 0),
        "hard_ids": draw_hard_ids(jax.random.fold_in(key_list[3], 71), 0),
    }


SOFTMAX_TEMPER = 0.02
LOSS_SCALE = 64.0
EPSILON = 1e-06

def to_units(values):
    floats = values.astype(jnp.float32)
    scales = lax.rsqrt(lax.optimization_barrier(jnp.mean(floats * floats, -1, keepdims=True)) + EPSILON)
    return (floats, scales, (floats * scales).astype(jnp.bfloat16))

def norm_back(floats, scales, upstream):
    return scales * upstream - scales * scales * scales * floats * lax.optimization_barrier(jnp.mean(floats * upstream, -1, keepdims=True))

def reference(queries, passages, hard_ids):
    inverse_permutation = 1.0 / (EMBED_DIMENSION * SOFTMAX_TEMPER)
    factor = LOSS_SCALE * inverse_permutation
    row_index = jnp.arange(PAIRS).astype(jnp.int32)
    grp_of = row_index // PAIRS_DEV % N_GRP
    targets_all = ((hard_ids // PAIRS_DEV * N_GRP + grp_of) * PAIRS_DEV + hard_ids % PAIRS_DEV).astype(jnp.int32)
    query_groups = queries.reshape(N_BATCH, GROUP, EMBED_DIMENSION)
    passage_groups = passages.reshape(N_BATCH, GROUP, EMBED_DIMENSION)
    target_groups = targets_all.reshape(N_BATCH, GROUP)
    positive = (jnp.arange(GROUP)[:, None] == jnp.arange(GROUP)[None, :]).astype(jnp.float32)

    def first_pass(running, inputs):
        query_raw, passage_raw, target_labels = inputs
        qfloat, qscale, qshort = to_units(query_raw)
        pfloat, pscale, pshort = to_units(passage_raw)
        hard_float, hard_scale, hard_short = to_units(jnp.take(passages, target_labels, axis=0))
        inner_scores = jnp.dot(qshort, pshort.T, preferred_element_type=jnp.float32) * inverse_permutation
        hard_score = lax.optimization_barrier(jnp.sum(qshort.astype(jnp.float32) * hard_short.astype(jnp.float32), 1)) * inverse_permutation
        totals = jnp.log(lax.optimization_barrier(jnp.sum(jnp.exp(inner_scores), 1)) + jnp.exp(hard_score))
        inner_w = (jnp.exp(inner_scores - totals[:, None]) - positive).astype(jnp.bfloat16)
        hard_w = jnp.exp(hard_score - totals).astype(jnp.bfloat16).astype(jnp.float32)
        unit_q = (jnp.dot(inner_w, pshort, preferred_element_type=jnp.float32) + hard_w[:, None] * hard_short.astype(jnp.float32)) * factor
        qgrad = norm_back(qfloat, qscale, unit_q).astype(jnp.bfloat16)
        grad_terms = hard_w[:, None] * qshort.astype(jnp.float32) * factor
        running = running.at[target_labels].add(grad_terms)
        return (running, (qgrad, totals))
    spread, (qgrad_groups, total_groups) = lax.scan(first_pass, jnp.zeros((PAIRS, EMBED_DIMENSION), jnp.float32), (query_groups, passage_groups, target_groups))

    def second_pass(inputs):
        query_raw, passage_raw, totals, spread_group = inputs
        qfloat, qscale, qshort = to_units(query_raw)
        pfloat, pscale, pshort = to_units(passage_raw)
        inner_scores = jnp.dot(qshort, pshort.T, preferred_element_type=jnp.float32) * inverse_permutation
        inner_w = (jnp.exp(inner_scores - totals[:, None]) - positive).astype(jnp.bfloat16)
        unit_p = jnp.dot(inner_w.T, qshort, preferred_element_type=jnp.float32) * factor + spread_group
        return norm_back(pfloat, pscale, unit_p).astype(jnp.bfloat16)
    passage_gradient_groups = lax.map(second_pass, (query_groups, passage_groups, total_groups, spread.reshape(N_BATCH, GROUP, EMBED_DIMENSION)))
    return (qgrad_groups.reshape(PAIRS, EMBED_DIMENSION), passage_gradient_groups.reshape(PAIRS, EMBED_DIMENSION))
```

```python
import functools

import jax
import jax.numpy as jnp
from jax import lax
from jax.experimental import pallas as pl
from jax.experimental.pallas import tpu as pltpu
from jax.sharding import PartitionSpec as P

SOFTMAX_TEMPER = 0.02
LOSS_SCALE = 64.0
EPSILON = 1e-06

PLANES = 16
PLANE = 8
FAR = PLANES // 2
SLOTS = 2
OWN = PLANE * SLOTS
CAPS = [0, 84, 76, 68, 60, 50, 38, 24, 8, 0]
LANES = 128


def row_scales(values):
    floats = values.astype(jnp.float32)
    return lax.rsqrt(jnp.mean(floats * floats, -1, keepdims=True) + EPSILON)


def norm_back(values, scales, upstream):
    floats = values.astype(jnp.float32)
    return scales * upstream - scales * scales * scales * floats * jnp.mean(
        floats * upstream, -1, keepdims=True
    )


def offsets_of(sizes):
    out, total = [], 0
    for size in sizes:
        out.append(total)
        total += size
    return out, total


OUT_AT, OUT_ROWS = offsets_of([0] + [CAPS[d] for d in range(1, FAR + 1)])
CAP1 = CAPS[1]


def exchange_kernel(
    inv, srv, mrg, pick, fin,
    q3, p3, qs, ps,
    hard, owed, gp, gq,
    out, final, qfirst, pstage, qstage,
    own_sem, x_send, x_recv, qz_send, qz_recv, pz_send, pz_recv,
    py_send, py_recv, qy_send, qy_recv, *arriving
):
    comb = [[None, *arriving[s * FAR : (s + 1) * FAR]] for s in range(2)]
    qin = [[None, *arriving[(2 + s) * FAR : (3 + s) * FAR]] for s in range(2)]
    rows = q3.shape[0]
    half = rows // 2
    b = lax.axis_index("batch")
    g = lax.axis_index("grp")
    n_grp = 4
    z, me = b // PLANE, b % PLANE

    def plane(step):
        return lax.rem(z + step + PLANES, PLANES)

    def peer(j):
        return lax.rem(me + j, PLANE)

    ahead = [{"batch": plane(1) * PLANE + me}, {"batch": plane(-1) * PLANE + me}]
    right, left = lax.rem(g + 1, n_grp), lax.rem(g + n_grp - 1, n_grp)
    sides = [{"grp": right}, {"grp": left}]
    peers = [{"batch": z * PLANE + peer(j)} for j in range(1, PLANE)]

    barrier = pltpu.get_barrier_semaphore()
    greeted = ahead + sides + peers
    for device in greeted:
        pl.semaphore_signal(barrier, inc=1, device_id=device, device_id_type=pl.DeviceIdType.MESH)
    pl.semaphore_wait(barrier, len(greeted))

    def remote(src, dst, send, recv, device):
        return pltpu.make_async_remote_copy(
            src_ref=src, dst_ref=dst, send_sem=send, recv_sem=recv,
            device_id=device, device_id_type=pl.DeviceIdType.MESH,
        )

    def block(ref, who, start=0, size=rows):
        return ref.at[pl.ds(pl.multiple_of(who * rows + start, half), size), :]

    whole = ((ps, gp), (qs, gq))
    locals_ = []
    for a, (src, dst) in enumerate(whole):
        copy = pltpu.make_async_copy(src, block(dst, g), own_sem.at[a])
        copy.start()
        locals_.append(copy)
        for s in range(2):
            remote(src, block(dst, g), x_send.at[a, s], x_recv.at[a, s], sides[s]).start()

    def pass_on(a):
        dst = whole[a][1]
        for s, origin in ((0, left), (1, right)):
            remote(ps, block(dst, origin), x_send.at[a, s], x_recv.at[a, s], sides[s]).wait_recv()
            part = block(dst, origin, s * half, half)
            remote(part, part, x_send.at[a, 2 + s], x_recv.at[a, 2 + s], sides[s]).start()

    def x_end(a):
        dst = whole[a][1]
        across = lax.rem(g + 2, n_grp)
        for s in range(2):
            part = block(dst, across, s * half, half)
            remote(part, part, x_send.at[a, 2 + s], x_recv.at[a, 2 + s], sides[s]).wait()
            remote(ps, block(dst, g), x_send.at[a, s], x_recv.at[a, s], sides[s]).wait_send()

    def copy_rows(n, store, load):
        def body(r, carry):
            store(r, load(r))
            return carry

        lax.fori_loop(0, n, body, 0, unroll=False)

    def q_hop(s, d):
        if d == 1:
            src = qfirst.at[s]
        else:
            src = qin[s][d - 1].at[pl.ds(0, CAPS[d])]
        return remote(
            src, qin[s][d], qz_send.at[s, d], qz_recv.at[s, d], ahead[1 - s]
        )

    for s in range(2):
        def store(r, value, s=s):
            qfirst[s, r] = value

        def load(r, s=s):
            return q3[inv[s, r]]

        copy_rows(CAP1, store, load)
        q_hop(s, 1).start()

    def p_owed(s, d):
        return plane(d) if s == 0 else plane(-d)

    def partners(s, d):
        return range(s, PLANE, 2) if d == FAR else range(PLANE)

    def p_spread(s, d):
        target = p_owed(s, d)
        place = pl.ds(me * SLOTS, SLOTS)
        others = 0
        for j in partners(s, d):
            for k in range(SLOTS):
                row = p3[srv[target * PLANE + peer(j), k]]
                if j == 0:
                    comb[s][d][me * SLOTS + k] = row
                else:
                    pstage[s, d, others * SLOTS + k] = row
            if j:
                others += 1
        others = 0
        for j in partners(s, d):
            if j:
                remote(
                    pstage.at[s, d, pl.ds(others * SLOTS, SLOTS)], comb[s][d].at[place],
                    py_send.at[s, d], py_recv.at[s, d], peers[j - 1],
                ).start()
                others += 1

    def p_spread_near():
        near = 2 * CAP1
        for k in range(SLOTS):
            final[near + me * SLOTS + k] = p3[srv[z * PLANE + me, k]]
        for j in range(1, PLANE):
            for k in range(SLOTS):
                pstage[0, 0, (j - 1) * SLOTS + k] = p3[srv[z * PLANE + peer(j), k]]
        for j in range(1, PLANE):
            remote(
                pstage.at[0, 0, pl.ds((j - 1) * SLOTS, SLOTS)],
                final.at[pl.ds(near + me * SLOTS, SLOTS)],
                py_send.at[0, 0], py_recv.at[0, 0], peers[j - 1],
            ).start()

    def spread_bytes(s, d):
        n = SLOTS * len([j for j in partners(s, d) if j])
        return pstage.at[s, d, pl.ds(0, n)]

    for d in range(FAR, 0, -1):
        for s in range(2):
            p_spread(s, d)
    p_spread_near()

    def p_hop(s, d):
        src = out.at[s, pl.ds(OUT_AT[d], CAPS[d])]
        if d == 1:
            dst = final.at[pl.ds(s * CAP1, CAP1)]
        else:
            dst = comb[s][d - 1].at[pl.ds(OWN, CAPS[d])]
        return remote(src, dst, pz_send.at[s, d], pz_recv.at[s, d], ahead[s])

    def p_step(s, d):
        here = spread_bytes(s, d)
        pltpu.make_async_copy(here, here, py_recv.at[s, d]).wait()
        if d < FAR:
            p_hop(s, d + 1).wait_recv()
        target = p_owed(s, d)

        def store(r, value):
            out[s, OUT_AT[d] + r] = value

        def load(r):
            return comb[s][d][mrg[target, s, r]]

        copy_rows(CAPS[d], store, load)
        p_hop(s, d).start()

    def q_spread(s, d):
        source = plane(d) if s == 0 else plane(-d)

        def take(j, k):
            at = pick[source, peer(j) * SLOTS + k]
            if d == 0:
                return q3[at]
            return qin[j % 2 if d == FAR else s][d][at]

        place = (source * PLANE + me) * SLOTS
        line = 2 * d + s
        for j in range(PLANE):
            for k in range(SLOTS):
                qstage[line, j * SLOTS + k] = take(j, k)
        pltpu.make_async_copy(
            qstage.at[line, pl.ds(0, SLOTS)], owed.at[pl.ds(place, SLOTS)], own_sem.at[2 + line]
        ).start()
        for j in range(1, PLANE):
            remote(
                qstage.at[line, pl.ds(j * SLOTS, SLOTS)], owed.at[pl.ds(place, SLOTS)],
                qy_send.at[line], qy_recv.at[line], peers[j - 1],
            ).start()

    q_spread(0, 0)
    for step in range(1, FAR + 1):
        for s in range(2):
            q_hop(s, step).wait_recv()
            if step < FAR:
                q_hop(s, step + 1).start()
        for s in range(2):
            p_step(s, FAR + 1 - step)
        for s in range(2):
            if step < FAR or s == 0:
                q_spread(s, step)
        if step == 2:
            pass_on(0)
        if step == 4:
            pass_on(1)

    for s in range(2):
        p_hop(s, 1).wait_recv()
    here = spread_bytes(0, 0)
    pltpu.make_async_copy(here, here, py_recv.at[0, 0]).wait()

    def store(r, value):
        hard[r] = value

    def load(r):
        return final[fin[r]]

    copy_rows(rows, store, load)

    x_end(0)
    x_end(1)
    for copy in locals_:
        copy.wait()
    for d in range(FAR + 1):
        for s in range(2):
            if (d == 0 or d == FAR) and s == 1:
                continue
            line = 2 * d + s
            sent = qstage.at[line, pl.ds(SLOTS, OWN - SLOTS)]
            pltpu.make_async_copy(sent, sent, qy_send.at[line]).wait()
            pltpu.make_async_copy(sent, sent, qy_recv.at[line]).wait()
            pltpu.make_async_copy(
                qstage.at[line, pl.ds(0, SLOTS)], owed.at[pl.ds(0, SLOTS)], own_sem.at[2 + line]
            ).wait()
    for d in range(FAR + 1):
        for s in range(2):
            if d == 0 and s == 1:
                continue
            here = spread_bytes(s, d)
            pltpu.make_async_copy(here, here, py_send.at[s, d]).wait()
            if d > 0:
                q_hop(s, d).wait_send()
                p_hop(s, d).wait_send()


def exchange(inv, srv, mrg, pick, fin, q3, p3, qs, ps):
    rows, width = qs.shape
    line = (width // LANES, LANES)
    slot_total = PLANES * PLANE * SLOTS
    smem = pl.BlockSpec(memory_space=pltpu.SMEM)
    vmem = pl.BlockSpec(memory_space=pltpu.VMEM)
    hbm = pl.BlockSpec(memory_space=pl.ANY)
    dma = pltpu.SemaphoreType.DMA

    def buffer(*lead):
        return pltpu.VMEM(lead + line, jnp.bfloat16)

    return pl.pallas_call(
        exchange_kernel,
        out_shape=(
            jax.ShapeDtypeStruct((rows,) + line, jnp.bfloat16),
            jax.ShapeDtypeStruct((slot_total,) + line, jnp.bfloat16),
            jax.ShapeDtypeStruct((4 * rows, width), jnp.bfloat16),
            jax.ShapeDtypeStruct((4 * rows, width), jnp.bfloat16),
        ),
        in_specs=[smem] * 5 + [vmem, vmem, hbm, hbm],
        out_specs=(vmem, vmem, hbm, hbm),
        scratch_shapes=[
            buffer(2, OUT_ROWS),
            buffer(2 * CAP1 + OWN),
            buffer(2, CAP1),
            buffer(2, FAR + 1, OWN),
            buffer(2 * (FAR + 1), OWN),
            dma((2 + 2 * (FAR + 1),)),
            dma((2, 4)), dma((2, 4)),
            dma((2, FAR + 1)), dma((2, FAR + 1)),
            dma((2, FAR + 1)), dma((2, FAR + 1)),
            dma((2, FAR + 1)), dma((2, FAR + 1)),
            dma((2 * (FAR + 1),)), dma((2 * (FAR + 1),)),
            *[buffer(OWN + CAPS[d + 1]) for _ in range(2) for d in range(1, FAR + 1)],
            *[buffer(CAPS[d]) for _ in range(2) for d in range(1, FAR + 1)],
        ],
        compiler_params=pltpu.CompilerParams(
            collective_id=0, has_side_effects=True, vmem_limit_bytes=60 * 1024 * 1024
        ),
        cost_estimate=pl.CostEstimate(flops=0, bytes_accessed=40 * 1024 * 1024, transcendentals=0),
        name="exchange",
    )(inv, srv, mrg, pick, fin, q3, p3, qs, ps)


def column_kernel(x, full, here, plane_send, plane_recv, z_send, z_recv):
    b = lax.axis_index("batch")
    z, me = b // PLANE, b % PLANE
    peers = [{"batch": z * PLANE + lax.rem(me + j, PLANE)} for j in range(1, PLANE)]
    lines = [{"batch": lax.rem(z + j, PLANES) * PLANE + me} for j in range(1, PLANES)]
    barrier = pltpu.get_barrier_semaphore()
    for device in peers + lines:
        pl.semaphore_signal(barrier, inc=1, device_id=device, device_id_type=pl.DeviceIdType.MESH)
    pl.semaphore_wait(barrier, len(peers + lines))

    def send(src, dst, sems, device):
        pltpu.make_async_remote_copy(
            src_ref=src, dst_ref=dst, send_sem=sems[0].at[0], recv_sem=sems[1].at[0],
            device_id=device, device_id_type=pl.DeviceIdType.MESH,
        ).start()

    def settle(rows, sem):
        ref = full.at[pl.ds(0, rows)]
        pltpu.make_async_copy(ref, ref, sem.at[0]).wait()

    full[b] = x[...]
    here[0] = x[...]
    for device in peers:
        send(here.at[0], full.at[b], (plane_send, plane_recv), device)
    settle(PLANE - 1, plane_recv)
    mine = full.at[pl.ds(z * PLANE, PLANE)]
    for device in lines:
        send(mine, mine, (z_send, z_recv), device)
    settle(PLANE * (PLANES - 1), z_recv)
    settle(PLANE - 1, plane_send)
    settle(PLANE * (PLANES - 1), z_send)


def column(x, collective_id, name):
    rows = x.shape[0]
    dma = pltpu.SemaphoreType.DMA((1,))
    full = pl.pallas_call(
        column_kernel,
        out_shape=jax.ShapeDtypeStruct((PLANES * PLANE, 1, rows), x.dtype),
        in_specs=[pl.BlockSpec(memory_space=pltpu.VMEM)],
        out_specs=pl.BlockSpec(memory_space=pltpu.VMEM),
        scratch_shapes=[pltpu.VMEM((1, 1, rows), x.dtype), dma, dma, dma, dma],
        compiler_params=pltpu.CompilerParams(collective_id=collective_id, has_side_effects=True),
        name=name,
    )(x.reshape(1, rows))
    return full.reshape(PLANES * PLANE, rows)


def course(ahead, owner_me, me):
    tie = (owner_me + me) % 2
    side = jnp.where(ahead == 0, 2, jnp.where(ahead < FAR, 0, jnp.where(ahead == FAR, tie, 1)))
    return side, jnp.where(ahead <= FAR, ahead, PLANES - ahead)


def too_many(ids_all, rows):
    who = jnp.arange(PLANES * PLANE)
    owner = ids_all // rows
    ahead = (who[:, None] // PLANE - owner // PLANE + PLANES) % PLANES
    side, dist = course(ahead, owner % PLANE, (who % PLANE)[:, None])
    hops = jnp.arange(2 * FAR)
    caps = jnp.zeros((2 * FAR,), jnp.int32)
    for d in range(1, FAR + 1):
        caps = jnp.where(hops % FAR == d - 1, CAPS[d], caps)
    uses = (side[:, None, :] == hops[None, :, None] // FAR) & (dist[:, None, :] > hops[None, :, None] % FAR)
    need = jnp.sum(uses.astype(jnp.int32), 2)
    return jnp.max(jnp.where(need > caps[None, :], 1, 0)) > 0


def tables(ids_all, b, rows):
    z, me = b // PLANE, b % PLANE
    r = jnp.arange(rows)
    planes = jnp.arange(PLANES)
    line = lax.dynamic_slice_in_dim(ids_all.reshape(PLANES, PLANE, rows), me, 1, 1)[:, 0]
    owner = line // rows
    oz, om = owner // PLANE, owner % PLANE
    earlier = r[None, :] < r[:, None]
    slot = jnp.sum(((owner[:, :, None] == owner[:, None, :]) & earlier).astype(jnp.int32), 2)
    ahead = (planes[:, None] - oz + PLANES) % PLANES
    side, dist = course(ahead, om, me)
    key = dist * rows + (rows - 1 - r)[None, :]
    before = (side[:, :, None] == side[:, None, :]) & (key[:, None, :] > key[:, :, None])
    pos = jnp.sum(before.astype(jnp.int32), 2)
    cell = om * SLOTS + slot
    mine = oz == z

    at = jnp.arange(CAP1)
    sides = jnp.arange(2)
    hit = (side[:, None, None, :] == sides[None, :, None, None]) & (
        pos[:, None, None, :] == at[None, None, :, None]
    )
    placed = jnp.max(jnp.where(hit & mine[:, None, None, :], cell[:, None, None, :], -1), 3)
    far = jnp.stack([(planes - z + PLANES) % PLANES, (z - planes + PLANES) % PLANES], 1)
    room = jnp.zeros_like(far)
    for d in range(1, FAR):
        room = jnp.where(far == d, CAPS[d + 1], room)
    filler = SLOTS * ((me + sides) % PLANE)
    other = jnp.where(at[None, None, :] < room[:, :, None], OWN + at[None, None, :], filler[None, :, None])
    mrg = jnp.where(placed >= 0, placed, other)

    cells = jnp.arange(OWN)
    place = jnp.where(side == 2, r[None, :], pos)
    pick = jnp.sum(
        jnp.where(mine[:, None, :] & (cell[:, None, :] == cells[None, :, None]), place[:, None, :], 0), 2
    )

    def own(values):
        return lax.dynamic_slice_in_dim(values, z, 1, 0)[0]

    my_side, my_pos, my_cell = own(side), own(pos), own(cell)
    inv = jnp.sum(
        jnp.where(
            (my_side[None, None, :] == sides[:, None, None]) & (my_pos[None, None, :] == at[None, :, None]),
            r[None, None, :], 0,
        ), 2,
    )
    fin = jnp.where(my_side == 2, 2 * CAP1 + my_cell, my_side * CAP1 + my_pos)

    wanted = ids_all // rows == b
    code = r[None, :] * rows + ids_all % rows
    count = jnp.sum(wanted.astype(jnp.int32), 1)
    first = jnp.min(jnp.where(wanted, code, rows * rows), 1)
    last = jnp.max(jnp.where(wanted, code, 0), 1)
    first = jnp.where(count > 0, first, 0)
    codes = jnp.stack([first, last], 1)
    used = jnp.stack([count > 0, count > 1], 1)
    return inv, codes % rows, mrg, pick, fin, codes // rows, used, own(owner) * SLOTS + own(slot)


def padded(qshort, pshort, srv, home):
    rows, width = qshort.shape
    count = PLANES * PLANE

    def swap(values):
        moved = lax.all_to_all(
            values.reshape(count, SLOTS, width), "batch", split_axis=0, concat_axis=0, tiled=True
        )
        return moved.reshape(count * SLOTS, width)

    hard = jnp.take(swap(jnp.take(pshort, srv.reshape(-1), axis=0)), home, axis=0)
    sender = jnp.sum(
        jnp.where(jnp.arange(count * SLOTS)[:, None] == home[None, :], jnp.arange(rows)[None, :], 0), 1
    )
    return hard, swap(jnp.take(qshort, sender, axis=0))


def local(queries, passages, hard_ids):
    pair_rows, embedding_dimension = queries.shape
    batch_count = lax.axis_size("batch")
    group_rows = lax.axis_size("grp") * pair_rows
    group_pos = lax.axis_index("grp")
    scale = 1.0 / (embedding_dimension * SOFTMAX_TEMPER)
    factor = LOSS_SCALE * scale
    line = (pair_rows, embedding_dimension // LANES, LANES)

    ids_all = column(hard_ids, 1, "hard_ids_column")
    qscale = row_scales(queries)
    pscale = row_scales(passages)
    qshort = (queries.astype(jnp.float32) * qscale).astype(jnp.bfloat16)
    pshort = (passages.astype(jnp.float32) * pscale).astype(jnp.bfloat16)
    inv, srv, mrg, pick, fin, asker_row, used, home = tables(ids_all, lax.axis_index("batch"), pair_rows)
    hard3, owed3, group_p, group_q = exchange(
        inv, srv, mrg, pick, fin, qshort.reshape(line), pshort.reshape(line), qshort, pshort
    )
    hard_p, owed = lax.cond(
        too_many(ids_all, pair_rows),
        lambda: padded(qshort, pshort, srv, home),
        lambda: (hard3.reshape(pair_rows, embedding_dimension), owed3.reshape(-1, embedding_dimension)),
    )

    local_rows = jnp.arange(pair_rows)
    own_cols = group_pos * pair_rows + local_rows
    positive = (jnp.arange(group_rows)[None, :] == own_cols[:, None]).astype(jnp.float32)
    inner_scores = jnp.dot(qshort, group_p.T, preferred_element_type=jnp.float32) * scale
    hard_score = jnp.sum(qshort.astype(jnp.float32) * hard_p.astype(jnp.float32), 1) * scale
    totals = jnp.log(jnp.sum(jnp.exp(inner_scores), 1) + jnp.exp(hard_score))
    hard_w = jnp.exp(hard_score - totals).astype(jnp.bfloat16)
    group_totals = lax.all_gather(totals, "grp", axis=0, tiled=True)
    weights_all = column(hard_w.astype(jnp.float32), 2, "weights_column")

    inner_w = (jnp.exp(inner_scores - totals[:, None]) - positive).astype(jnp.bfloat16)
    unit_q = (
        jnp.dot(inner_w, group_p, preferred_element_type=jnp.float32)
        + hard_w.astype(jnp.float32)[:, None] * hard_p
    ) * factor
    query_grad = norm_back(queries, qscale, unit_q).astype(jnp.bfloat16)

    asked = asker_row[:, :, None] == local_rows[None, None, :]
    slot_w = jnp.sum(jnp.where(asked & used[:, :, None], weights_all[:, None, :], 0.0), 2).reshape(-1)
    spread_w = jnp.where(local_rows[:, None] == srv.reshape(-1)[None, :], slot_w[None, :], 0.0)
    scores = jnp.dot(group_q, pshort.T, preferred_element_type=jnp.float32) * scale
    inner_t = (jnp.exp(scores - group_totals[:, None]) - positive.T).astype(jnp.bfloat16)
    unit_p = (
        jnp.dot(inner_t.T, group_q, preferred_element_type=jnp.float32)
        + jnp.dot(spread_w.astype(jnp.bfloat16), owed, preferred_element_type=jnp.float32)
    ) * factor
    passage_grad = norm_back(passages, pscale, unit_p).astype(jnp.bfloat16)
    return (query_grad, passage_grad)


def solution(mesh):
    in_specs = (P(("batch", "grp"), None), P(("batch", "grp"), None), P(("batch", "grp")))
    out_specs = (P(("batch", "grp"), None), P(("batch", "grp"), None))
    return jax.shard_map(local, mesh=mesh, in_specs=in_specs, out_specs=out_specs, check_vma=False)
```

```python
import functools

import jax
import jax.numpy as jnp
from jax import lax
from jax.experimental import pallas as pl
from jax.experimental.pallas import tpu as pltpu
from jax.sharding import PartitionSpec as P

SOFTMAX_TEMPER = 0.02
LOSS_SCALE = 64.0
EPSILON = 1e-06

PLANES = 16
PLANE = 8
FAR = PLANES // 2
SLOTS = 2
OWN = PLANE * SLOTS
CAPS = [0, 84, 76, 68, 60, 50, 38, 24, 8, 0]
LANES = 128
LAG = 2


def row_scales(values):
    floats = values.astype(jnp.float32)
    return lax.rsqrt(jnp.mean(floats * floats, -1, keepdims=True) + EPSILON)


def norm_back(values, scales, upstream):
    floats = values.astype(jnp.float32)
    return scales * upstream - scales * scales * scales * floats * jnp.mean(
        floats * upstream, -1, keepdims=True
    )


def offsets_of(sizes):
    out, total = [], 0
    for size in sizes:
        out.append(total)
        total += size
    return out, total


OUT_AT, OUT_ROWS = offsets_of([0] + [CAPS[d] for d in range(1, FAR + 1)])
CAP1 = CAPS[1]


def exchange_kernel(
    inv, srv, mrg, pick, fin,
    q3, p3, qs, ps, queries, passages, qscale, pscale, asked, flag,
    query_grad, passage_grad, flags,
    gp, gq, out, final, qfirst, pstage, qstage, owed, floats, unit, scores, scores_t,
    ends, gathered, weights, sums,
    own_sem, x_send, x_recv, qz_send, qz_recv, pz_send, pz_recv,
    py_send, py_recv, qy_send, qy_recv, t_send, t_recv, c_send, c_recv, *arriving
):
    comb = [[None, *arriving[s * FAR : (s + 1) * FAR]] for s in range(2)]
    qin = [[None, *arriving[(2 + s) * FAR : (3 + s) * FAR]] for s in range(2)]
    rows = q3.shape[0]
    half = rows // 2
    b = lax.axis_index("batch")
    g = lax.axis_index("grp")
    n_grp = 4
    z, me = b // PLANE, b % PLANE

    def plane(step):
        return lax.rem(z + step + PLANES, PLANES)

    def peer(j):
        return lax.rem(me + j, PLANE)

    lines = [{"batch": plane(j) * PLANE + me} for j in range(1, PLANES)]
    ahead = [lines[0], lines[-1]]
    right, left = lax.rem(g + 1, n_grp), lax.rem(g + n_grp - 1, n_grp)
    sides = [{"grp": right}, {"grp": left}]
    peers = [{"batch": z * PLANE + peer(j)} for j in range(1, PLANE)]

    barrier = pltpu.get_barrier_semaphore()
    across = lax.rem(g + 2, n_grp)
    sides.append({"grp": across})
    greeted = lines + sides + peers
    for device in greeted:
        pl.semaphore_signal(barrier, inc=1, device_id=device, device_id_type=pl.DeviceIdType.MESH)
    pl.semaphore_wait(barrier, len(greeted))

    def remote(src, dst, send, recv, device):
        return pltpu.make_async_remote_copy(
            src_ref=src, dst_ref=dst, send_sem=send, recv_sem=recv,
            device_id=device, device_id_type=pl.DeviceIdType.MESH,
        )

    def block(ref, who, start=0, size=rows):
        return ref.at[pl.ds(pl.multiple_of(who * rows + start, half), size), :]

    whole = ((ps, gp), (qs, gq))
    locals_ = []
    for a, (src, dst) in enumerate(whole):
        copy = pltpu.make_async_copy(src, block(dst, g), own_sem.at[a])
        copy.start()
        locals_.append(copy)
        for s in range(2):
            remote(src, block(dst, g), x_send.at[a, s], x_recv.at[a, s], sides[s]).start()

    def pass_on(a):
        dst = whole[a][1]
        for s, origin in ((0, left), (1, right)):
            remote(ps, block(dst, origin), x_send.at[a, s], x_recv.at[a, s], sides[s]).wait_recv()
            part = block(dst, origin, s * half, half)
            remote(part, part, x_send.at[a, 2 + s], x_recv.at[a, 2 + s], sides[s]).start()

    def x_end(a):
        dst = whole[a][1]
        for s in range(2):
            part = block(dst, across, s * half, half)
            remote(part, part, x_send.at[a, 2 + s], x_recv.at[a, 2 + s], sides[s]).wait()
            remote(ps, block(dst, g), x_send.at[a, s], x_recv.at[a, s], sides[s]).wait_send()

    def copy_rows(n, store, load):
        def body(r, carry):
            store(r, load(r))
            return carry

        lax.fori_loop(0, n, body, 0, unroll=False)

    def q_hop(s, d):
        if d == 1:
            src = qfirst.at[s]
        else:
            src = qin[s][d - 1].at[pl.ds(0, CAPS[d])]
        return remote(
            src, qin[s][d], qz_send.at[s, d], qz_recv.at[s, d], ahead[1 - s]
        )

    for s in range(2):
        def store(r, value, s=s):
            qfirst[s, r] = value

        def load(r, s=s):
            return q3[inv[s, r]]

        copy_rows(CAP1, store, load)
        q_hop(s, 1).start()

    def p_owed(s, d):
        return plane(d) if s == 0 else plane(-d)

    def partners(s, d):
        return range(s, PLANE, 2) if d == FAR else range(PLANE)

    def p_spread(s, d):
        target = p_owed(s, d)
        place = pl.ds(me * SLOTS, SLOTS)
        others = 0
        for j in partners(s, d):
            for k in range(SLOTS):
                row = p3[srv[target * PLANE + peer(j), k]]
                if j == 0:
                    comb[s][d][me * SLOTS + k] = row
                else:
                    pstage[s, d, others * SLOTS + k] = row
            if j:
                others += 1
        others = 0
        for j in partners(s, d):
            if j:
                remote(
                    pstage.at[s, d, pl.ds(others * SLOTS, SLOTS)], comb[s][d].at[place],
                    py_send.at[s, d], py_recv.at[s, d], peers[j - 1],
                ).start()
                others += 1

    def p_spread_near():
        near = 2 * CAP1
        for k in range(SLOTS):
            final[near + me * SLOTS + k] = p3[srv[z * PLANE + me, k]]
        for j in range(1, PLANE):
            for k in range(SLOTS):
                pstage[0, 0, (j - 1) * SLOTS + k] = p3[srv[z * PLANE + peer(j), k]]
        for j in range(1, PLANE):
            remote(
                pstage.at[0, 0, pl.ds((j - 1) * SLOTS, SLOTS)],
                final.at[pl.ds(near + me * SLOTS, SLOTS)],
                py_send.at[0, 0], py_recv.at[0, 0], peers[j - 1],
            ).start()

    def spread_bytes(s, d):
        n = SLOTS * len([j for j in partners(s, d) if j])
        return pstage.at[s, d, pl.ds(0, n)]

    for d in range(FAR, 0, -1):
        for s in range(2):
            p_spread(s, d)
    p_spread_near()

    def p_hop(s, d):
        src = out.at[s, pl.ds(OUT_AT[d], CAPS[d])]
        if d == 1:
            dst = final.at[pl.ds(s * CAP1, CAP1)]
        else:
            dst = comb[s][d - 1].at[pl.ds(OWN, CAPS[d])]
        return remote(src, dst, pz_send.at[s, d], pz_recv.at[s, d], ahead[s])

    def p_step(s, d):
        here = spread_bytes(s, d)
        pltpu.make_async_copy(here, here, py_recv.at[s, d]).wait()
        if d < FAR:
            p_hop(s, d + 1).wait_recv()
        target = p_owed(s, d)

        def store(r, value):
            out[s, OUT_AT[d] + r] = value

        def load(r):
            return comb[s][d][mrg[target, s, r]]

        copy_rows(CAPS[d], store, load)
        p_hop(s, d).start()

    def q_spread(s, d):
        source = plane(d) if s == 0 else plane(-d)

        def take(j, k):
            at = pick[source, peer(j) * SLOTS + k]
            if d == 0:
                return q3[at]
            return qin[j % 2 if d == FAR else s][d][at]

        place = owed.at[:, me, source]
        line = 2 * d + s
        for j in range(PLANE):
            for k in range(SLOTS):
                qstage[line, j * SLOTS + k] = take(j, k)
        pltpu.make_async_copy(
            qstage.at[line, pl.ds(0, SLOTS)], place, own_sem.at[2 + line]
        ).start()
        for j in range(1, PLANE):
            remote(
                qstage.at[line, pl.ds(j * SLOTS, SLOTS)], place,
                qy_send.at[line], qy_recv.at[line], peers[j - 1],
            ).start()

    def q_step(d):
        for s in range(2):
            q_hop(s, d).wait_recv()
            if d < FAR:
                q_hop(s, d + 1).start()
        for s in range(2):
            if d < FAR or s == 0:
                q_spread(s, d)

    width = qs.shape[1]
    scale = 1.0 / (width * SOFTMAX_TEMPER)
    factor = LOSS_SCALE * scale
    lanes_per_row = width // LANES

    def columns(i, size):
        return pl.ds(pl.multiple_of(i * size, size), size)

    def score(dst, a, others):
        dst[...] = jnp.zeros_like(dst)
        chunk = 512

        def body(i, carry):
            at = columns(i, chunk)
            dst[...] += lax.dot_general(
                a[:, at], others[:, at], (((1,), (1,)), ((), ())), preferred_element_type=jnp.float32
            )
            return carry

        lax.fori_loop(0, width // chunk, body, 0)
        dst[...] = dst[...] * scale

    def laid_out(k, n):
        return floats[pl.ds(k, n, stride=lanes_per_row), :]

    def as_row(column_values):
        return jnp.transpose(jnp.broadcast_to(column_values, (rows, rows)))[0:1, :]

    def finish(values, scales, dots, result):
        scale_col = scales[...]
        weight = scale_col * scale_col * scale_col * (jnp.sum(dots, 1, keepdims=True) / width)

        def body(i, carry):
            at = columns(i, 256)
            result[:, at] = (
                scale_col * unit[:, at] - weight * values[:, at].astype(jnp.float32)
            ).astype(jnp.bfloat16)
            return carry

        lax.fori_loop(0, width // 256, body, 0)

    def product(weight_rows, group):
        def body(i, carry):
            at = columns(i, 256)
            unit[:, at] = jnp.dot(weight_rows, group[:, at], preferred_element_type=jnp.float32)
            return carry

        lax.fori_loop(0, width // 256, body, 0)

    q_spread(0, 0)
    for step in range(1, FAR + 1):
        for s in range(2):
            p_step(s, FAR + 1 - step)
        if step > LAG:
            q_step(step - LAG)
        if step == 2:
            pass_on(0)
        if step == 3:
            pass_on(1)
        if step == 5:
            x_end(0)
            for copy in locals_:
                copy.wait()
            score(scores, qs, gp)
            sums[...] = jnp.sum(jnp.exp(scores[...]), 1, keepdims=True)
        if step == 6:
            x_end(1)
            score(scores_t, ps, gq)

    for s in range(2):
        p_hop(s, 1).wait_recv()
    here = spread_bytes(0, 0)
    pltpu.make_async_copy(here, here, py_recv.at[0, 0]).wait()

    def store(r, value):
        floats[pl.ds(pl.multiple_of(r * lanes_per_row, lanes_per_row), lanes_per_row), :] = value.astype(
            jnp.float32
        )

    def load(r):
        return final[fin[r]]

    copy_rows(rows, store, load)

    dots = jnp.zeros((rows, LANES), jnp.float32)
    for k in range(lanes_per_row):
        dots += laid_out(k, rows) * qs[:, k * LANES : (k + 1) * LANES].astype(jnp.float32)
    hard_score = jnp.sum(dots, 1, keepdims=True) * scale
    totals = jnp.log(sums[...] + jnp.exp(hard_score))
    hard_w = jnp.exp(hard_score - totals).astype(jnp.bfloat16).astype(jnp.float32)

    ends[g, 0] = as_row(totals)
    ends[g, 1] = flag[...]
    weights[me, z] = as_row(hard_w)
    t_copies = [remote(ends.at[g], ends.at[g], t_send.at[i], t_recv.at[i], sides[i]) for i in range(3)]
    for copy in t_copies:
        copy.start()
    own_row = weights.at[me, z]
    for device in lines:
        remote(own_row, own_row, c_send.at[0], c_recv.at[0], device).start()

    def settle(ref, sem):
        pltpu.make_async_copy(ref, ref, sem).wait()

    for d in range(FAR - LAG + 1, FAR):
        q_step(d)

    row_at = lax.broadcasted_iota(jnp.int32, scores.shape, 0)
    col_at = lax.broadcasted_iota(jnp.int32, scores.shape, 1)
    positive = jnp.where(col_at == row_at + g * rows, 1.0, 0.0)
    product((jnp.exp(scores[...] - totals) - positive).astype(jnp.bfloat16), gp)
    dots = jnp.zeros((rows, LANES), jnp.float32)
    for k in range(lanes_per_row):
        at = slice(k * LANES, (k + 1) * LANES)
        value = (unit[:, at] + hard_w * laid_out(k, rows)) * factor
        unit[:, at] = value
        dots += queries[:, at].astype(jnp.float32) * value
    finish(queries, qscale, dots, query_grad)

    settle(weights.at[0, pl.ds(0, PLANES - 1)], c_recv.at[0])
    own_line = weights.at[me]
    for device in peers:
        remote(own_line, own_line, c_send.at[1], c_recv.at[1], device).start()
    q_step(FAR)

    for copy in t_copies:
        copy.wait()
    group_totals = jnp.concatenate([ends[i, 0] for i in range(n_grp)], axis=1)
    flags[...] = jnp.maximum(jnp.maximum(ends[0, 1], ends[1, 1]), jnp.maximum(ends[2, 1], ends[3, 1]))
    product((jnp.exp(scores_t[...] - group_totals) - positive).astype(jnp.bfloat16), gq)

    settle(weights.at[pl.ds(0, PLANE - 1)], c_recv.at[1])
    for who in range(PLANE):
        for at in range(PLANES):
            gathered[pl.ds(who * PLANES + at, 1), :] = weights[who, at]
    lane = lax.broadcasted_iota(jnp.int32, (rows, LANES), 1)
    placed = []
    for k in range(SLOTS):
        asker, offset = asked[:, 2 * k : 2 * k + 1], asked[:, 2 * k + 1 : 2 * k + 2]
        slot_w = jnp.sum(jnp.where(lane == asker, gathered[...], 0.0), 1, keepdims=True)
        placed.append(jnp.transpose(jnp.where(lane == offset, slot_w, 0.0)))
    spread_w = jnp.concatenate(placed, axis=1).astype(jnp.bfloat16)

    for d in range(FAR + 1):
        for s in range(2):
            if (d == 0 or d == FAR) and s == 1:
                continue
            line = 2 * d + s
            sent = qstage.at[line, pl.ds(SLOTS, OWN - SLOTS)]
            settle(sent, qy_recv.at[line])
            settle(qstage.at[line, pl.ds(0, SLOTS)], own_sem.at[2 + line])

    for k in range(SLOTS):
        for who in range(PLANE):
            base = (k * PLANE + who) * PLANES * lanes_per_row

            def widen(r, carry, k=k, who=who, base=base):
                at = pl.multiple_of(base + r * lanes_per_row, lanes_per_row)
                floats[pl.ds(at, lanes_per_row), :] = owed[k, who, r].astype(jnp.float32)
                return carry

            lax.fori_loop(0, PLANES, widen, 0)
    dots = jnp.zeros((rows, LANES), jnp.float32)
    for k in range(0, lanes_per_row, 2):
        at = slice(k * LANES, (k + 2) * LANES)
        pair = jnp.concatenate([laid_out(k, SLOTS * rows), laid_out(k + 1, SLOTS * rows)], axis=1)
        value = unit[:, at] + jnp.dot(spread_w, pair.astype(jnp.bfloat16), preferred_element_type=jnp.float32)
        value = value * factor
        unit[:, at] = value
        both = passages[:, at].astype(jnp.float32) * value
        dots += both[:, :LANES] + both[:, LANES:]
    finish(passages, pscale, dots, passage_grad)

    settle(weights.at[0, pl.ds(0, PLANES - 1)], c_send.at[0])
    settle(weights.at[pl.ds(0, PLANE - 1)], c_send.at[1])
    for d in range(FAR + 1):
        for s in range(2):
            if (d == 0 or d == FAR) and s == 1:
                continue
            line = 2 * d + s
            settle(qstage.at[line, pl.ds(SLOTS, OWN - SLOTS)], qy_send.at[line])
    for d in range(FAR + 1):
        for s in range(2):
            if d == 0 and s == 1:
                continue
            here = spread_bytes(s, d)
            pltpu.make_async_copy(here, here, py_send.at[s, d]).wait()
            if d > 0:
                q_hop(s, d).wait_send()
                p_hop(s, d).wait_send()


def exchange(tables_, *arrays):
    rows, width = arrays[2].shape
    line = (width // LANES, LANES)
    smem = pl.BlockSpec(memory_space=pltpu.SMEM)
    vmem = pl.BlockSpec(memory_space=pltpu.VMEM)
    dma = pltpu.SemaphoreType.DMA

    def buffer(*lead):
        return pltpu.VMEM(lead + line, jnp.bfloat16)

    def wide(*shape):
        return pltpu.VMEM(shape, jnp.float32)

    return pl.pallas_call(
        exchange_kernel,
        out_shape=(
            jax.ShapeDtypeStruct((rows, width), jnp.bfloat16),
            jax.ShapeDtypeStruct((rows, width), jnp.bfloat16),
            jax.ShapeDtypeStruct((1, LANES), jnp.float32),
        ),
        in_specs=[smem] * 5 + [vmem] * 10,
        out_specs=(vmem, vmem, vmem),
        scratch_shapes=[
            pltpu.VMEM((4 * rows, width), jnp.bfloat16),
            pltpu.VMEM((4 * rows, width), jnp.bfloat16),
            buffer(2, OUT_ROWS),
            buffer(2 * CAP1 + OWN),
            buffer(2, CAP1),
            buffer(2, FAR + 1, OWN),
            buffer(2 * (FAR + 1), OWN),
            buffer(SLOTS, PLANE, PLANES),
            wide(SLOTS * rows * line[0], LANES),
            wide(rows, width),
            wide(rows, 4 * rows),
            wide(rows, 4 * rows),
            wide(4, 2, 1, LANES),
            wide(PLANE * PLANES, LANES),
            wide(PLANE, PLANES, 1, LANES),
            wide(rows, 1),
            dma((2 + 2 * (FAR + 1),)),
            dma((2, 4)), dma((2, 4)),
            dma((2, FAR + 1)), dma((2, FAR + 1)),
            dma((2, FAR + 1)), dma((2, FAR + 1)),
            dma((2, FAR + 1)), dma((2, FAR + 1)),
            dma((2 * (FAR + 1),)), dma((2 * (FAR + 1),)),
            dma((3,)), dma((3,)),
            dma((2,)), dma((2,)),
            *[buffer(OWN + CAPS[d + 1]) for _ in range(2) for d in range(1, FAR + 1)],
            *[buffer(CAPS[d]) for _ in range(2) for d in range(1, FAR + 1)],
        ],
        compiler_params=pltpu.CompilerParams(
            collective_id=0, has_side_effects=True, vmem_limit_bytes=62 * 1024 * 1024
        ),
        cost_estimate=pl.CostEstimate(
            flops=2 * 2 * 2 * rows * 4 * rows * width, bytes_accessed=8 * 1024 * 1024, transcendentals=0
        ),
        name="exchange",
    )(*tables_, *arrays)


def column_kernel(x, full, here, plane_send, plane_recv, z_send, z_recv):
    b = lax.axis_index("batch")
    z, me = b // PLANE, b % PLANE
    peers = [{"batch": z * PLANE + lax.rem(me + j, PLANE)} for j in range(1, PLANE)]
    lines = [{"batch": lax.rem(z + j, PLANES) * PLANE + me} for j in range(1, PLANES)]
    barrier = pltpu.get_barrier_semaphore()
    for device in peers + lines:
        pl.semaphore_signal(barrier, inc=1, device_id=device, device_id_type=pl.DeviceIdType.MESH)
    pl.semaphore_wait(barrier, len(peers + lines))

    def send(src, dst, sems, device):
        pltpu.make_async_remote_copy(
            src_ref=src, dst_ref=dst, send_sem=sems[0].at[0], recv_sem=sems[1].at[0],
            device_id=device, device_id_type=pl.DeviceIdType.MESH,
        ).start()

    def settle(rows, sem):
        ref = full.at[pl.ds(0, rows)]
        pltpu.make_async_copy(ref, ref, sem.at[0]).wait()

    full[b] = x[...]
    here[0] = x[...]
    for device in peers:
        send(here.at[0], full.at[b], (plane_send, plane_recv), device)
    settle(PLANE - 1, plane_recv)
    mine = full.at[pl.ds(z * PLANE, PLANE)]
    for device in lines:
        send(mine, mine, (z_send, z_recv), device)
    settle(PLANE * (PLANES - 1), z_recv)
    settle(PLANE - 1, plane_send)
    settle(PLANE * (PLANES - 1), z_send)


def column(x, collective_id, name):
    rows = x.shape[0]
    dma = pltpu.SemaphoreType.DMA((1,))
    full = pl.pallas_call(
        column_kernel,
        out_shape=jax.ShapeDtypeStruct((PLANES * PLANE, 1, rows), x.dtype),
        in_specs=[pl.BlockSpec(memory_space=pltpu.VMEM)],
        out_specs=pl.BlockSpec(memory_space=pltpu.VMEM),
        scratch_shapes=[pltpu.VMEM((1, 1, rows), x.dtype), dma, dma, dma, dma],
        compiler_params=pltpu.CompilerParams(collective_id=collective_id, has_side_effects=True),
        name=name,
    )(x.reshape(1, rows))
    return full.reshape(PLANES * PLANE, rows)


def course(ahead, owner_me, me):
    tie = (owner_me + me) % 2
    side = jnp.where(ahead == 0, 2, jnp.where(ahead < FAR, 0, jnp.where(ahead == FAR, tie, 1)))
    return side, jnp.where(ahead <= FAR, ahead, PLANES - ahead)


def too_many(ids_all, rows):
    who = jnp.arange(PLANES * PLANE)
    owner = ids_all // rows
    ahead = (who[:, None] // PLANE - owner // PLANE + PLANES) % PLANES
    side, dist = course(ahead, owner % PLANE, (who % PLANE)[:, None])
    hops = jnp.arange(2 * FAR)
    caps = jnp.zeros((2 * FAR,), jnp.int32)
    for d in range(1, FAR + 1):
        caps = jnp.where(hops % FAR == d - 1, CAPS[d], caps)
    uses = (side[:, None, :] == hops[None, :, None] // FAR) & (dist[:, None, :] > hops[None, :, None] % FAR)
    need = jnp.sum(uses.astype(jnp.int32), 2)
    return jnp.max(jnp.where(need > caps[None, :], 1, 0)) > 0


def tables(ids_all, b, rows):
    z, me = b // PLANE, b % PLANE
    r = jnp.arange(rows)
    planes = jnp.arange(PLANES)
    line = lax.dynamic_slice_in_dim(ids_all.reshape(PLANES, PLANE, rows), me, 1, 1)[:, 0]
    owner = line // rows
    oz, om = owner // PLANE, owner % PLANE
    earlier = r[None, :] < r[:, None]
    slot = jnp.sum(((owner[:, :, None] == owner[:, None, :]) & earlier).astype(jnp.int32), 2)
    ahead = (planes[:, None] - oz + PLANES) % PLANES
    side, dist = course(ahead, om, me)
    key = dist * rows + (rows - 1 - r)[None, :]
    before = (side[:, :, None] == side[:, None, :]) & (key[:, None, :] > key[:, :, None])
    pos = jnp.sum(before.astype(jnp.int32), 2)
    cell = om * SLOTS + slot
    mine = oz == z

    at = jnp.arange(LANES)
    sides = jnp.arange(2)
    hit = (side[:, None, None, :] == sides[None, :, None, None]) & (
        pos[:, None, None, :] == at[None, None, :, None]
    )
    placed = jnp.max(jnp.where(hit & mine[:, None, None, :], cell[:, None, None, :], -1), 3)
    far = jnp.stack([(planes - z + PLANES) % PLANES, (z - planes + PLANES) % PLANES], 1)
    room = jnp.zeros_like(far)
    for d in range(1, FAR):
        room = jnp.where(far == d, CAPS[d + 1], room)
    filler = SLOTS * ((me + sides) % PLANE)
    other = jnp.where(at[None, None, :] < room[:, :, None], OWN + at[None, None, :], filler[None, :, None])
    mrg = jnp.where(placed >= 0, placed, other)

    cells = jnp.arange(OWN)
    place = jnp.where(side == 2, r[None, :], pos)
    pick = jnp.sum(
        jnp.where(mine[:, None, :] & (cell[:, None, :] == cells[None, :, None]), place[:, None, :], 0), 2
    )

    def own(values):
        return lax.dynamic_slice_in_dim(values, z, 1, 0)[0]

    my_side, my_pos, my_cell = own(side), own(pos), own(cell)
    inv = jnp.sum(
        jnp.where(
            (my_side[None, None, :] == sides[:, None, None]) & (my_pos[None, None, :] == at[None, :, None]),
            r[None, None, :], 0,
        ), 2,
    )
    fin = jnp.where(my_side == 2, 2 * CAP1 + my_cell, my_side * CAP1 + my_pos)

    wanted = ids_all // rows == b
    code = r[None, :] * rows + ids_all % rows
    count = jnp.sum(wanted.astype(jnp.int32), 1)
    first = jnp.min(jnp.where(wanted, code, rows * rows), 1)
    last = jnp.max(jnp.where(wanted, code, 0), 1)
    first = jnp.where(count > 0, first, 0)
    codes = jnp.stack([first, last], 1)
    used = jnp.stack([count > 0, count > 1], 1)
    asker = jnp.where(used, codes // rows, -1)
    asked = jnp.stack([asker[:, 0], codes[:, 0] % rows, asker[:, 1], codes[:, 1] % rows], 1)
    asked = asked.reshape(PLANES, PLANE, 4).transpose(1, 0, 2).reshape(-1, 4)
    return inv, codes % rows, mrg, pick, fin, asked


def padded(queries, passages, hard_ids):
    pair_rows, embedding_dimension = queries.shape
    batch_count = lax.axis_size("batch")
    group_number_total = lax.axis_size("grp")
    group_pos = lax.axis_index("grp")
    capacity = 2 * ((pair_rows + batch_count - 1) // batch_count)
    slot_total = batch_count * capacity
    group_rows = group_number_total * pair_rows
    inverse_permutation = 1.0 / (embedding_dimension * SOFTMAX_TEMPER)
    factor = LOSS_SCALE * inverse_permutation
    qscale = row_scales(queries)
    pscale = row_scales(passages)
    qshort = (queries.astype(jnp.float32) * qscale).astype(jnp.bfloat16)
    pshort = (passages.astype(jnp.float32) * pscale).astype(jnp.bfloat16)
    owners = hard_ids // pair_rows
    offsets = hard_ids % pair_rows
    local_rows = jnp.arange(pair_rows)
    same_owner = owners[:, None] == owners[None, :]
    earlier = local_rows[:, None] > local_rows[None, :]
    rank_in = jnp.sum((same_owner & earlier).astype(jnp.int32), 1)
    slot_index = owners * capacity + rank_in
    slot_table = jnp.arange(slot_total)[:, None] == slot_index[None, :]
    requests = jnp.sum(jnp.where(slot_table, offsets[None, :], 0), 1)
    requests = requests.reshape(batch_count, capacity)
    served_req = lax.all_to_all(requests, "batch", split_axis=0, concat_axis=0, tiled=True)
    served_flat = served_req.reshape(-1)
    served = jnp.take(pshort, served_flat, axis=0).reshape(
        batch_count, capacity, embedding_dimension
    )
    arrived = lax.all_to_all(served, "batch", split_axis=0, concat_axis=0, tiled=True)
    hard_p = jnp.take(arrived.reshape(slot_total, embedding_dimension), slot_index, axis=0)
    group_p, group_q = (
        lax.all_gather(pshort, "grp", axis=0, tiled=True),
        lax.all_gather(qshort, "grp", axis=0, tiled=True),
    )
    own_cols = group_pos * pair_rows + local_rows
    positive = (jnp.arange(group_rows)[None, :] == own_cols[:, None]).astype(jnp.float32)
    inner_scores = (
        jnp.dot(qshort, group_p.T, preferred_element_type=jnp.float32) * inverse_permutation
    )
    hard_score = (
        jnp.einsum("rd,rd->r", qshort, hard_p, preferred_element_type=jnp.float32)
        * inverse_permutation
    )
    totals = jnp.log(jnp.sum(jnp.exp(inner_scores), 1) + jnp.exp(hard_score))
    inner_w = (jnp.exp(inner_scores - totals[:, None]) - positive).astype(jnp.bfloat16)
    hard_w = jnp.exp(hard_score - totals).astype(jnp.bfloat16)
    unit_q = (
        jnp.dot(inner_w, group_p, preferred_element_type=jnp.float32)
        + hard_w.astype(jnp.float32)[:, None] * hard_p
    ) * factor
    query_grad = norm_back(queries, qscale, unit_q).astype(jnp.bfloat16)
    group_totals = lax.all_gather(totals, "grp", axis=0, tiled=True)
    scores = jnp.dot(group_q, pshort.T, preferred_element_type=jnp.float32) * inverse_permutation
    weight_factors = (jnp.exp(scores - group_totals[:, None]) - positive.T).astype(jnp.bfloat16)
    unit_p = jnp.dot(weight_factors.T, group_q, preferred_element_type=jnp.float32) * factor
    return_table = local_rows[:, None] == served_flat[None, :]
    own_terms = hard_w.astype(jnp.float32)[:, None] * qshort * factor
    term_slots = jnp.dot(
        slot_table.astype(jnp.float32),
        own_terms,
        precision=lax.Precision.HIGHEST,
        preferred_element_type=jnp.float32,
    )
    grad_terms = lax.all_to_all(
        term_slots.reshape(batch_count, capacity, embedding_dimension).astype(jnp.bfloat16),
        "batch",
        split_axis=0,
        concat_axis=0,
        tiled=True,
    ).astype(jnp.float32)
    spread = jnp.dot(
        return_table.astype(jnp.float32),
        grad_terms.reshape(slot_total, embedding_dimension),
        precision=lax.Precision.HIGHEST,
        preferred_element_type=jnp.float32,
    )
    passage_grad = norm_back(passages, pscale, unit_p + spread).astype(jnp.bfloat16)
    return (query_grad, passage_grad)


def local(queries, passages, hard_ids):
    pair_rows, embedding_dimension = queries.shape
    line = (pair_rows, embedding_dimension // LANES, LANES)
    b = lax.axis_index("batch")

    ids_all = column(hard_ids, 1, "hard_ids_column")
    qscale = row_scales(queries)
    pscale = row_scales(passages)
    qshort = (queries.astype(jnp.float32) * qscale).astype(jnp.bfloat16)
    pshort = (passages.astype(jnp.float32) * pscale).astype(jnp.bfloat16)
    inv, srv, mrg, pick, fin, asked = tables(ids_all, b, pair_rows)
    over = jnp.broadcast_to(too_many(ids_all, pair_rows).astype(jnp.float32), (1, LANES))
    query_grad, passage_grad, flags = exchange(
        (inv, srv, mrg, pick, fin),
        qshort.reshape(line), pshort.reshape(line), qshort, pshort,
        queries, passages, qscale, pscale, asked, over,
    )
    return lax.cond(
        flags[0, 0] > 0,
        lambda: padded(queries, passages, hard_ids),
        lambda: (query_grad, passage_grad),
    )


def solution(mesh):
    in_specs = (P(("batch", "grp"), None), P(("batch", "grp"), None), P(("batch", "grp")))
    out_specs = (P(("batch", "grp"), None), P(("batch", "grp"), None))
    return jax.shard_map(local, mesh=mesh, in_specs=in_specs, out_specs=out_specs, check_vma=False)
```

```python
import functools

import jax
import jax.numpy as jnp
from jax import lax
from jax.experimental import pallas as pl
from jax.experimental.pallas import tpu as pltpu
from jax.sharding import PartitionSpec as P

SOFTMAX_TEMPER = 0.02
LOSS_SCALE = 64.0
EPSILON = 1e-06

PLANES = 16
PLANE = 8
FAR = PLANES // 2
SLOTS = 2
OWN = PLANE * SLOTS
CAPS = [0, 84, 76, 68, 60, 50, 38, 24, 8, 0]
LANES = 128
Q_AT = {1: (2,), 3: (3,), 5: (4,), 6: (5,), 7: (6,)}


def row_scales(values):
    floats = values.astype(jnp.float32)
    return lax.rsqrt(jnp.mean(floats * floats, -1, keepdims=True) + EPSILON)


def norm_back(values, scales, upstream):
    floats = values.astype(jnp.float32)
    return scales * upstream - scales * scales * scales * floats * jnp.mean(
        floats * upstream, -1, keepdims=True
    )


def offsets_of(sizes):
    out, total = [], 0
    for size in sizes:
        out.append(total)
        total += size
    return out, total


OUT_AT, OUT_ROWS = offsets_of([0] + [CAPS[d] for d in range(1, FAR + 1)])
CAP1 = CAPS[1]
SPLIT = 40


def parts_of(d):
    return [c for c in range(2) if CAPS[d] > c * SPLIT]


def part_of(d, c):
    return c * SPLIT, (CAPS[d] - SPLIT if c else min(CAPS[d], SPLIT))


def exchange_kernel(
    ids, queries, passages,
    query_grad, passage_grad, flags,
    q3, p3, qs, ps, qscale, pscale, column_ids, ids2, line_table, own_table, slot_table, asked,
    line_at, own_at, slot_at,
    gp, gq, out, final, qfirst, pstage, qstage, owed, floats, unit, scores, scores_t,
    ends, gathered, weights, sums,
    own_sem, x_send, x_recv, qz_send, qz_recv, pz_send, pz_recv,
    py_send, py_recv, qy_send, qy_recv, t_send, t_recv, c_send, c_recv, i_send, i_recv, table_sem, *arriving
):
    own = [[None, *arriving[(4 + s) * FAR : (5 + s) * FAR]] for s in range(2)]
    comb = [[None, *arriving[s * FAR : (s + 1) * FAR]] for s in range(2)]
    qin = [[None, *arriving[(2 + s) * FAR : (3 + s) * FAR]] for s in range(2)]
    rows, width = queries.shape
    lanes_per_row = width // LANES
    half = rows // 2
    b = lax.axis_index("batch")
    g = lax.axis_index("grp")
    n_grp = 4
    z, me = b // PLANE, b % PLANE

    def plane(step):
        return lax.rem(z + step + PLANES, PLANES)

    def peer(j):
        return lax.rem(me + j, PLANE)

    lines = [{"batch": plane(j) * PLANE + me} for j in range(1, PLANES)]
    ahead = [lines[0], lines[-1]]
    right, left = lax.rem(g + 1, n_grp), lax.rem(g + n_grp - 1, n_grp)
    sides = [{"grp": right}, {"grp": left}]
    peers = [{"batch": z * PLANE + peer(j)} for j in range(1, PLANE)]

    barrier = pltpu.get_barrier_semaphore()
    across = lax.rem(g + 2, n_grp)
    sides.append({"grp": across})
    greeted = lines + sides + peers
    for device in greeted:
        pl.semaphore_signal(barrier, inc=1, device_id=device, device_id_type=pl.DeviceIdType.MESH)

    def columns(i, size):
        return pl.ds(pl.multiple_of(i * size, size), size)

    def unit_rows(values, scales, short, spread):
        def square(i, total):
            part = values[:, columns(i, 256)].astype(jnp.float32)
            part = part * part
            return total + part[:, :LANES] + part[:, LANES:]

        total = lax.fori_loop(0, width // 256, square, jnp.zeros((rows, LANES), jnp.float32))
        scale_col = lax.rsqrt(jnp.sum(total, 1, keepdims=True) / width + EPSILON)
        scales[...] = scale_col
        for k in range(lanes_per_row):
            at = slice(k * LANES, (k + 1) * LANES)
            part = (values[:, at].astype(jnp.float32) * scale_col).astype(jnp.bfloat16)
            short[:, at] = part
            floats[pl.ds(k, rows, stride=lanes_per_row), :] = part.astype(jnp.float32)

        def narrow(r, carry):
            at = pl.ds(pl.multiple_of(r * lanes_per_row, lanes_per_row), lanes_per_row)
            spread[r] = floats[at, :].astype(jnp.bfloat16)
            return carry

        lax.fori_loop(0, rows, narrow, 0)

    sub = lax.broadcasted_iota(jnp.int32, (rows, LANES), 0)
    lane = lax.broadcasted_iota(jnp.int32, (rows, LANES), 1)

    def course_of(values, plane_of, me_of):
        oz, om = values >> 10, (values >> 7) & (PLANE - 1)
        ahead_of = (plane_of - oz) & (PLANES - 1)
        tie = (om + me_of) & 1
        side = jnp.where(ahead_of == 0, 2, jnp.where(ahead_of < FAR, 0, jnp.where(ahead_of == FAR, tie, 1)))
        return oz, om, side, jnp.where(ahead_of <= FAR, ahead_of, PLANES - ahead_of)

    def as_column(row):
        wide_row = jnp.broadcast_to(row.astype(jnp.float32), (rows, rows))
        return jnp.transpose(wide_row).astype(jnp.int32)

    def count_lanes(mask):
        return jnp.sum(jnp.where(mask, 1.0, 0.0), 1, keepdims=True).astype(jnp.int32)

    def pick_row(mask, values):
        return jnp.sum(jnp.where(mask, values.astype(jnp.float32), 0.0), 0, keepdims=True).astype(jnp.int32)

    def requests(row, plane_of):
        row = jnp.broadcast_to(row, (rows, LANES))
        col = as_column(row[0:1])
        _, _, side_r, dist_r = course_of(row, plane_of, me)
        oz, om, side, dist = course_of(col, plane_of, me)
        code_r = dist_r * LANES + (LANES - 1) - lane
        code = dist * LANES + (LANES - 1) - sub
        pos = count_lanes((side_r == side) & (code_r > code))
        slot = count_lanes(((row >> 7) == (col >> 7)) & (lane < sub))
        return oz, side, jnp.broadcast_to(pos, (rows, LANES)), om * SLOTS + jnp.minimum(slot, SLOTS - 1)

    unit_rows(queries, qscale, qs, q3)
    _, my_side, my_pos, my_cell = requests(ids[...], z)
    for s in range(2):
        own_table[s : s + 1, :] = jnp.minimum(pick_row((my_side == s) & (my_pos == lane), sub), rows - 1)
    home = jnp.where(my_side == 2, 2 * CAP1 + my_cell, my_side * CAP1 + jnp.minimum(my_pos, CAP1 - 1))
    own_table[2:3, :] = pick_row(sub == lane, home)
    own_copy = pltpu.make_async_copy(own_table, own_at, table_sem.at[0])
    own_copy.start()
    column_ids[b] = ids[...]
    pl.semaphore_wait(barrier, len(greeted))

    def remote(src, dst, send, recv, device):
        return pltpu.make_async_remote_copy(
            src_ref=src, dst_ref=dst, send_sem=send, recv_sem=recv,
            device_id=device, device_id_type=pl.DeviceIdType.MESH,
        )

    def settle(ref, sem):
        pltpu.make_async_copy(ref, ref, sem).wait()

    own_ids = column_ids.at[b]
    for device in peers:
        remote(own_ids, own_ids, i_send.at[0], i_recv.at[0], device).start()

    def block(ref, who, start=0, size=rows):
        return ref.at[pl.ds(pl.multiple_of(who * rows + start, half), size), :]

    whole = ((ps, gp), (qs, gq))
    locals_ = []

    def pass_on(a):
        dst = whole[a][1]
        for s, origin in ((0, left), (1, right)):
            remote(ps, block(dst, origin), x_send.at[a, s], x_recv.at[a, s], sides[s]).wait_recv()
            part = block(dst, origin, s * half, half)
            remote(part, part, x_send.at[a, 2 + s], x_recv.at[a, 2 + s], sides[s]).start()

    def x_end(a):
        dst = whole[a][1]
        for s in range(2):
            part = block(dst, across, s * half, half)
            remote(part, part, x_send.at[a, 2 + s], x_recv.at[a, 2 + s], sides[s]).wait()
            remote(ps, block(dst, g), x_send.at[a, s], x_recv.at[a, s], sides[s]).wait_send()

    def inside(at, count):
        return jnp.maximum(jnp.minimum(at, count - 1), 0)

    def copy_rows(n, store, load):
        def body(r, carry):
            store(r, load(r))
            return carry

        lax.fori_loop(0, n, body, 0, unroll=False)

    def q_hop(s, d, c):
        low, size = part_of(d, c)
        src = qfirst.at[s] if d == 1 else qin[s][d - 1]
        at = pl.ds(low, size)
        return remote(src.at[at], qin[s][d].at[at], qz_send.at[s, d, c], qz_recv.at[s, d, c], ahead[1 - s])

    own_copy.wait()
    for s in range(2):
        def store(r, value, s=s):
            qfirst[s, r] = value

        def load(r, s=s):
            return q3[inside(own_at[s, r], rows)]

        copy_rows(CAP1, store, load)
        for c in parts_of(1):
            q_hop(s, 1, c).start()

    settle(column_ids.at[pl.ds(0, PLANE - 1)], i_recv.at[0])
    plane_ids = column_ids.at[pl.ds(z * PLANE, PLANE)]
    for device in lines:
        remote(plane_ids, plane_ids, i_send.at[1], i_recv.at[1], device).start()
    unit_rows(passages, pscale, ps, p3)

    for a, (src, dst) in enumerate(whole):
        copy = pltpu.make_async_copy(src, block(dst, g), own_sem.at[a])
        copy.start()
        locals_.append(copy)
        for s in range(2):
            remote(src, block(dst, g), x_send.at[a, s], x_recv.at[a, s], sides[s]).start()

    settle(column_ids.at[pl.ds(0, PLANE * (PLANES - 1))], i_recv.at[1])

    def flat(r, carry):
        ids2[pl.ds(r, 1), :] = column_ids[r]
        return carry

    lax.fori_loop(0, PLANES * PLANE, flat, 0)

    wanted = (ids2[...] >> 7) == b
    code = (lane * LANES + (ids2[...] & (LANES - 1))).astype(jnp.float32)
    asks = count_lanes(wanted)
    first = jnp.min(jnp.where(wanted, code, float(LANES * LANES)), 1, keepdims=True).astype(jnp.int32)
    last = jnp.max(jnp.where(wanted, code, 0.0), 1, keepdims=True).astype(jnp.int32)
    first = jnp.where(asks > 0, first, 0)
    askers = [jnp.where(asks > 0, first >> 7, -1), jnp.where(asks > 1, last >> 7, -1)]
    offsets = [first & (LANES - 1), last & (LANES - 1)]
    slot_table[...] = jnp.where(lane == 0, offsets[0], offsets[1])
    slot_copy = pltpu.make_async_copy(slot_table, slot_at, table_sem.at[1])
    slot_copy.start()
    asked[...] = jnp.where(
        lane == 0, askers[0], jnp.where(lane == 1, offsets[0], jnp.where(lane == 2, askers[1], offsets[1]))
    )

    def line_rows(source, carry):
        oz, side, pos, cell = requests(ids2[pl.ds(source * PLANE + me, 1), :], source)
        here = oz == z
        for s in range(2):
            hit = here & (side == s) & (pos == lane)
            placed = jnp.minimum(pick_row(hit, cell + 1) - 1, OWN - 1)
            far = lax.rem((source - z if s == 0 else z - source) + PLANES, PLANES)
            room = 0
            for d in range(1, FAR):
                room = jnp.where(far == d, CAPS[d + 1], room)
            filler = SLOTS * peer(s)
            other = jnp.where(lane[0:1] < room, OWN, filler)
            line_table[pl.ds(s * PLANES + source, 1), :] = jnp.where(placed >= 0, placed, other)
        place = jnp.where(side == 2, sub, pos)
        far = lax.rem(source - z + PLANES, PLANES)
        limit = rows - 1
        for d in range(1, FAR + 1):
            limit = jnp.where((far == d) | (far == PLANES - d), CAPS[d] - 1, limit)
        line_table[pl.ds(2 * PLANES + source, 1), :] = jnp.minimum(pick_row(here & (cell == lane), place), limit)
        return carry

    lax.fori_loop(0, PLANES, line_rows, 0)
    line_copy = pltpu.make_async_copy(line_table, line_at, table_sem.at[2])
    line_copy.start()
    slot_copy.wait()
    line_copy.wait()

    def p_owed(s, d):
        return plane(d) if s == 0 else plane(-d)

    def partners(s, d):
        return range(s, PLANE, 2) if d == FAR else range(PLANE)

    def p_spread(s, d):
        target = p_owed(s, d)
        place = pl.ds(me * SLOTS, SLOTS)
        others = 0
        for j in partners(s, d):
            for k in range(SLOTS):
                row = p3[inside(slot_at[target * PLANE + peer(j), k], rows)]
                if j == 0:
                    own[s][d][me * SLOTS + k] = row
                else:
                    pstage[s, d, others * SLOTS + k] = row
            if j:
                others += 1
        others = 0
        for j in partners(s, d):
            if j:
                remote(
                    pstage.at[s, d, pl.ds(others * SLOTS, SLOTS)], own[s][d].at[place],
                    py_send.at[s, d], py_recv.at[s, d], peers[j - 1],
                ).start()
                others += 1

    def p_spread_near():
        near = 2 * CAP1
        for k in range(SLOTS):
            final[near + me * SLOTS + k] = p3[inside(slot_at[z * PLANE + me, k], rows)]
        for j in range(1, PLANE):
            for k in range(SLOTS):
                pstage[0, 0, (j - 1) * SLOTS + k] = p3[inside(slot_at[z * PLANE + peer(j), k], rows)]
        for j in range(1, PLANE):
            remote(
                pstage.at[0, 0, pl.ds((j - 1) * SLOTS, SLOTS)],
                final.at[pl.ds(near + me * SLOTS, SLOTS)],
                py_send.at[0, 0], py_recv.at[0, 0], peers[j - 1],
            ).start()

    def spread_bytes(s, d):
        n = SLOTS * len([j for j in partners(s, d) if j])
        return pstage.at[s, d, pl.ds(0, n)]

    for d in range(FAR, 0, -1):
        for s in range(2):
            p_spread(s, d)
    p_spread_near()

    def p_hop(s, d, c):
        low, size = part_of(d, c)
        src = out.at[s, pl.ds(OUT_AT[d] + low, size)]
        dst = final.at[pl.ds(s * CAP1 + low, size)] if d == 1 else comb[s][d - 1].at[pl.ds(low, size)]
        return remote(src, dst, pz_send.at[s, d, c], pz_recv.at[s, d, c], ahead[s])

    def p_step(s, d, c):
        if c == 0:
            settle(spread_bytes(s, d), py_recv.at[s, d])
        low, size = part_of(d, c)
        target = p_owed(s, d)
        passing = 0
        if c in parts_of(d + 1):
            p_hop(s, d + 1, c).wait_recv()
            passing = part_of(d + 1, c)[1]

        def cell(r):
            return line_at[s * PLANES + target, r]

        def store(r, value):
            out[s, OUT_AT[d] + low + r] = value

        def load(r):
            at = cell(low + r)
            here = own[s][d][inside(at, OWN)]
            return lax.select(at < OWN, here, comb[s][d][low + r])

        copy_rows(passing, store, load)

        def store_new(r, value):
            out[s, OUT_AT[d] + low + passing + r] = value

        def load_new(r):
            return own[s][d][inside(cell(low + passing + r), OWN)]

        copy_rows(size - passing, store_new, load_new)
        p_hop(s, d, c).start()

    def q_spread(s, d):
        source = plane(d) if s == 0 else plane(-d)

        def take(j, k):
            at = line_at[2 * PLANES + source, peer(j) * SLOTS + k]
            if d == 0:
                return q3[inside(at, rows)]
            return qin[j % 2 if d == FAR else s][d][inside(at, CAPS[d])]

        place = owed.at[:, source, me]
        line = 2 * d + s
        for j in range(PLANE):
            for k in range(SLOTS):
                qstage[line, j * SLOTS + k] = take(j, k)
        pltpu.make_async_copy(
            qstage.at[line, pl.ds(0, SLOTS)], place, own_sem.at[2 + line]
        ).start()
        for j in range(1, PLANE):
            remote(
                qstage.at[line, pl.ds(j * SLOTS, SLOTS)], place,
                qy_send.at[line], qy_recv.at[line], peers[j - 1],
            ).start()

    def q_step(d):
        for c in parts_of(d):
            for s in range(2):
                q_hop(s, d, c).wait_recv()
                if c in parts_of(d + 1):
                    q_hop(s, d + 1, c).start()
        for s in range(2):
            if d < FAR or s == 0:
                q_spread(s, d)

    scale = 1.0 / (width * SOFTMAX_TEMPER)
    factor = LOSS_SCALE * scale

    def score(dst, a, others):
        dst[...] = jnp.zeros_like(dst)
        chunk = 512

        def body(i, carry):
            at = columns(i, chunk)
            dst[...] += lax.dot_general(
                a[:, at], others[:, at], (((1,), (1,)), ((), ())), preferred_element_type=jnp.float32
            )
            return carry

        lax.fori_loop(0, width // chunk, body, 0)
        dst[...] = dst[...] * scale

    def laid_out(k, n):
        return floats[pl.ds(k, n, stride=lanes_per_row), :]

    def as_row(column_values):
        return jnp.transpose(jnp.broadcast_to(column_values, (rows, rows)))[0:1, :]

    def finish(values, scales, dots, result):
        scale_col = scales[...]
        weight = scale_col * scale_col * scale_col * (jnp.sum(dots, 1, keepdims=True) / width)

        def body(i, carry):
            at = columns(i, 256)
            result[:, at] = (
                scale_col * unit[:, at] - weight * values[:, at].astype(jnp.float32)
            ).astype(jnp.bfloat16)
            return carry

        lax.fori_loop(0, width // 256, body, 0)

    def product(weight_rows, group):
        def body(i, carry):
            at = columns(i, 256)
            unit[:, at] = jnp.dot(weight_rows, group[:, at], preferred_element_type=jnp.float32)
            return carry

        lax.fori_loop(0, width // 256, body, 0)

    q_spread(0, 0)
    q_step(1)
    for step in range(1, FAR + 1):
        for c in parts_of(FAR + 1 - step):
            for s in range(2):
                p_step(s, FAR + 1 - step, c)
        for d in Q_AT.get(step, ()):
            q_step(d)
        if step == 2:
            pass_on(0)
        if step == 3:
            pass_on(1)
        if step == 5:
            x_end(0)
            for copy in locals_:
                copy.wait()
            score(scores, qs, gp)
            sums[...] = jnp.sum(jnp.exp(scores[...]), 1, keepdims=True)
        if step == 4:
            who = (sub >> 3, sub & (PLANE - 1))
            _, _, side, dist = course_of(ids2[...], *who)
            over = jnp.zeros((rows, 1), jnp.float32)
            for s in range(2):
                for d in range(1, FAR):
                    over = jnp.maximum(over, jnp.where(count_lanes((side == s) & (dist >= d)) > CAPS[d], 1.0, 0.0))
            flag = jnp.max(jnp.broadcast_to(over, (rows, LANES)), 0, keepdims=True)
        if step == 6:
            x_end(1)
            score(scores_t, ps, gq)

    for s in range(2):
        for c in parts_of(1):
            p_hop(s, 1, c).wait_recv()
    here = spread_bytes(0, 0)
    pltpu.make_async_copy(here, here, py_recv.at[0, 0]).wait()

    def store(r, value):
        floats[pl.ds(pl.multiple_of(r * lanes_per_row, lanes_per_row), lanes_per_row), :] = value.astype(
            jnp.float32
        )

    def load(r):
        return final[inside(own_at[2, r], 2 * CAP1 + OWN)]

    copy_rows(rows, store, load)

    dots = jnp.zeros((rows, LANES), jnp.float32)
    for k in range(lanes_per_row):
        dots += laid_out(k, rows) * qs[:, k * LANES : (k + 1) * LANES].astype(jnp.float32)
    hard_score = jnp.sum(dots, 1, keepdims=True) * scale
    totals = jnp.log(sums[...] + jnp.exp(hard_score))
    hard_w = jnp.exp(hard_score - totals).astype(jnp.bfloat16).astype(jnp.float32)

    ends[g, 0] = as_row(totals)
    ends[g, 1] = flag
    weights[me, z] = as_row(hard_w)
    t_copies = [remote(ends.at[g], ends.at[g], t_send.at[i], t_recv.at[i], sides[i]) for i in range(3)]
    for copy in t_copies:
        copy.start()
    own_row = weights.at[me, z]
    for device in lines:
        remote(own_row, own_row, c_send.at[0], c_recv.at[0], device).start()

    q_step(FAR - 1)

    row_at = lax.broadcasted_iota(jnp.int32, scores.shape, 0)
    col_at = lax.broadcasted_iota(jnp.int32, scores.shape, 1)
    positive = jnp.where(col_at == row_at + g * rows, 1.0, 0.0)
    product((jnp.exp(scores[...] - totals) - positive).astype(jnp.bfloat16), gp)
    dots = jnp.zeros((rows, LANES), jnp.float32)
    for k in range(lanes_per_row):
        at = slice(k * LANES, (k + 1) * LANES)
        value = (unit[:, at] + hard_w * laid_out(k, rows)) * factor
        unit[:, at] = value
        dots += queries[:, at].astype(jnp.float32) * value
    finish(queries, qscale, dots, query_grad)

    settle(weights.at[0, pl.ds(0, PLANES - 1)], c_recv.at[0])
    own_line = weights.at[me]
    for device in peers:
        remote(own_line, own_line, c_send.at[1], c_recv.at[1], device).start()
    q_step(FAR)

    for copy in t_copies:
        copy.wait()
    group_totals = jnp.concatenate([ends[i, 0] for i in range(n_grp)], axis=1)
    flags[...] = jnp.maximum(jnp.maximum(ends[0, 1], ends[1, 1]), jnp.maximum(ends[2, 1], ends[3, 1]))
    product((jnp.exp(scores_t[...] - group_totals) - positive).astype(jnp.bfloat16), gq)

    settle(weights.at[pl.ds(0, PLANE - 1)], c_recv.at[1])
    for who in range(PLANE):
        for at in range(PLANES):
            gathered[pl.ds(at * PLANE + who, 1), :] = weights[who, at]
    placed = []
    for k in range(SLOTS):
        asker, offset = asked[:, 2 * k : 2 * k + 1], asked[:, 2 * k + 1 : 2 * k + 2]
        slot_w = jnp.sum(jnp.where(lane == asker, gathered[...], 0.0), 1, keepdims=True)
        placed.append(jnp.transpose(jnp.where(lane == offset, slot_w, 0.0)))
    spread_w = jnp.concatenate(placed, axis=1).astype(jnp.bfloat16)

    for d in range(FAR + 1):
        for s in range(2):
            if (d == 0 or d == FAR) and s == 1:
                continue
            line = 2 * d + s
            sent = qstage.at[line, pl.ds(SLOTS, OWN - SLOTS)]
            settle(sent, qy_recv.at[line])
            settle(qstage.at[line, pl.ds(0, SLOTS)], own_sem.at[2 + line])

    for k in range(SLOTS):
        for who in range(PLANE):

            def widen(r, carry, k=k, who=who):
                at = pl.multiple_of(((k * PLANES + r) * PLANE + who) * lanes_per_row, lanes_per_row)
                floats[pl.ds(at, lanes_per_row), :] = owed[k, r, who].astype(jnp.float32)
                return carry

            lax.fori_loop(0, PLANES, widen, 0)
    dots = jnp.zeros((rows, LANES), jnp.float32)
    for k in range(0, lanes_per_row, 2):
        at = slice(k * LANES, (k + 2) * LANES)
        pair = jnp.concatenate([laid_out(k, SLOTS * rows), laid_out(k + 1, SLOTS * rows)], axis=1)
        value = unit[:, at] + jnp.dot(spread_w, pair.astype(jnp.bfloat16), preferred_element_type=jnp.float32)
        value = value * factor
        unit[:, at] = value
        both = passages[:, at].astype(jnp.float32) * value
        dots += both[:, :LANES] + both[:, LANES:]
    finish(passages, pscale, dots, passage_grad)

    settle(column_ids.at[pl.ds(0, PLANE - 1)], i_send.at[0])
    settle(column_ids.at[pl.ds(0, PLANE * (PLANES - 1))], i_send.at[1])
    settle(weights.at[0, pl.ds(0, PLANES - 1)], c_send.at[0])
    settle(weights.at[pl.ds(0, PLANE - 1)], c_send.at[1])
    for d in range(FAR + 1):
        for s in range(2):
            if (d == 0 or d == FAR) and s == 1:
                continue
            line = 2 * d + s
            settle(qstage.at[line, pl.ds(SLOTS, OWN - SLOTS)], qy_send.at[line])
    for d in range(FAR + 1):
        for s in range(2):
            if d == 0 and s == 1:
                continue
            here = spread_bytes(s, d)
            pltpu.make_async_copy(here, here, py_send.at[s, d]).wait()
            if d > 0:
                for c in parts_of(d):
                    q_hop(s, d, c).wait_send()
                    p_hop(s, d, c).wait_send()


def exchange(ids, queries, passages):
    rows, width = queries.shape
    line = (width // LANES, LANES)
    vmem = pl.BlockSpec(memory_space=pltpu.VMEM)
    dma = pltpu.SemaphoreType.DMA

    def buffer(*lead):
        return pltpu.VMEM(lead + line, jnp.bfloat16)

    def wide(*shape):
        return pltpu.VMEM(shape, jnp.float32)

    def table(*shape):
        return pltpu.VMEM(shape, jnp.int32)

    return pl.pallas_call(
        exchange_kernel,
        out_shape=(
            jax.ShapeDtypeStruct((rows, width), jnp.bfloat16),
            jax.ShapeDtypeStruct((rows, width), jnp.bfloat16),
            jax.ShapeDtypeStruct((1, LANES), jnp.float32),
        ),
        in_specs=[vmem] * 3,
        out_specs=(vmem, vmem, vmem),
        scratch_shapes=[
            buffer(rows),
            buffer(rows),
            pltpu.VMEM((rows, width), jnp.bfloat16),
            pltpu.VMEM((rows, width), jnp.bfloat16),
            wide(rows, 1),
            wide(rows, 1),
            table(PLANES * PLANE, 1, LANES),
            table(PLANES * PLANE, LANES),
            table(3 * PLANES, LANES),
            table(8, LANES),
            table(PLANES * PLANE, LANES),
            table(PLANES * PLANE, LANES),
            pltpu.SMEM((3 * PLANES, LANES), jnp.int32),
            pltpu.SMEM((8, LANES), jnp.int32),
            pltpu.SMEM((PLANES * PLANE, LANES), jnp.int32),
            pltpu.VMEM((4 * rows, width), jnp.bfloat16),
            pltpu.VMEM((4 * rows, width), jnp.bfloat16),
            buffer(2, OUT_ROWS),
            buffer(2 * CAP1 + OWN),
            buffer(2, CAP1),
            buffer(2, FAR + 1, OWN),
            buffer(2 * (FAR + 1), OWN),
            buffer(SLOTS, PLANES, PLANE),
            wide(SLOTS * rows * line[0], LANES),
            wide(rows, width),
            wide(rows, 4 * rows),
            wide(rows, 4 * rows),
            wide(4, 2, 1, LANES),
            wide(PLANE * PLANES, LANES),
            wide(PLANE, PLANES, 1, LANES),
            wide(rows, 1),
            dma((2 + 2 * (FAR + 1),)),
            dma((2, 4)), dma((2, 4)),
            dma((2, FAR + 1, 2)), dma((2, FAR + 1, 2)),
            dma((2, FAR + 1, 2)), dma((2, FAR + 1, 2)),
            dma((2, FAR + 1)), dma((2, FAR + 1)),
            dma((2 * (FAR + 1),)), dma((2 * (FAR + 1),)),
            dma((3,)), dma((3,)),
            dma((2,)), dma((2,)),
            dma((2,)), dma((2,)), dma((3,)),
            *[buffer(max(CAPS[d + 1], OWN)) for _ in range(2) for d in range(1, FAR + 1)],
            *[buffer(CAPS[d]) for _ in range(2) for d in range(1, FAR + 1)],
            *[buffer(OWN) for _ in range(2 * FAR)],
        ],
        compiler_params=pltpu.CompilerParams(
            collective_id=0, has_side_effects=True, vmem_limit_bytes=62 * 1024 * 1024
        ),
        cost_estimate=pl.CostEstimate(
            flops=2 * 2 * 2 * rows * 4 * rows * width, bytes_accessed=8 * 1024 * 1024, transcendentals=0
        ),
        name="exchange",
    )(ids, queries, passages)


def padded(queries, passages, hard_ids):
    pair_rows, embedding_dimension = queries.shape
    batch_count = lax.axis_size("batch")
    group_number_total = lax.axis_size("grp")
    group_pos = lax.axis_index("grp")
    capacity = 2 * ((pair_rows + batch_count - 1) // batch_count)
    slot_total = batch_count * capacity
    group_rows = group_number_total * pair_rows
    inverse_permutation = 1.0 / (embedding_dimension * SOFTMAX_TEMPER)
    factor = LOSS_SCALE * inverse_permutation
    qscale = row_scales(queries)
    pscale = row_scales(passages)
    qshort = (queries.astype(jnp.float32) * qscale).astype(jnp.bfloat16)
    pshort = (passages.astype(jnp.float32) * pscale).astype(jnp.bfloat16)
    owners = hard_ids // pair_rows
    offsets = hard_ids % pair_rows
    local_rows = jnp.arange(pair_rows)
    same_owner = owners[:, None] == owners[None, :]
    earlier = local_rows[:, None] > local_rows[None, :]
    rank_in = jnp.sum((same_owner & earlier).astype(jnp.int32), 1)
    slot_index = owners * capacity + rank_in
    slot_table = jnp.arange(slot_total)[:, None] == slot_index[None, :]
    requests = jnp.sum(jnp.where(slot_table, offsets[None, :], 0), 1)
    requests = requests.reshape(batch_count, capacity)
    served_req = lax.all_to_all(requests, "batch", split_axis=0, concat_axis=0, tiled=True)
    served_flat = served_req.reshape(-1)
    served = jnp.take(pshort, served_flat, axis=0).reshape(
        batch_count, capacity, embedding_dimension
    )
    arrived = lax.all_to_all(served, "batch", split_axis=0, concat_axis=0, tiled=True)
    hard_p = jnp.take(arrived.reshape(slot_total, embedding_dimension), slot_index, axis=0)
    group_p, group_q = (
        lax.all_gather(pshort, "grp", axis=0, tiled=True),
        lax.all_gather(qshort, "grp", axis=0, tiled=True),
    )
    own_cols = group_pos * pair_rows + local_rows
    positive = (jnp.arange(group_rows)[None, :] == own_cols[:, None]).astype(jnp.float32)
    inner_scores = (
        jnp.dot(qshort, group_p.T, preferred_element_type=jnp.float32) * inverse_permutation
    )
    hard_score = (
        jnp.einsum("rd,rd->r", qshort, hard_p, preferred_element_type=jnp.float32)
        * inverse_permutation
    )
    totals = jnp.log(jnp.sum(jnp.exp(inner_scores), 1) + jnp.exp(hard_score))
    inner_w = (jnp.exp(inner_scores - totals[:, None]) - positive).astype(jnp.bfloat16)
    hard_w = jnp.exp(hard_score - totals).astype(jnp.bfloat16)
    unit_q = (
        jnp.dot(inner_w, group_p, preferred_element_type=jnp.float32)
        + hard_w.astype(jnp.float32)[:, None] * hard_p
    ) * factor
    query_grad = norm_back(queries, qscale, unit_q).astype(jnp.bfloat16)
    group_totals = lax.all_gather(totals, "grp", axis=0, tiled=True)
    scores = jnp.dot(group_q, pshort.T, preferred_element_type=jnp.float32) * inverse_permutation
    weight_factors = (jnp.exp(scores - group_totals[:, None]) - positive.T).astype(jnp.bfloat16)
    unit_p = jnp.dot(weight_factors.T, group_q, preferred_element_type=jnp.float32) * factor
    return_table = local_rows[:, None] == served_flat[None, :]
    own_terms = hard_w.astype(jnp.float32)[:, None] * qshort * factor
    term_slots = jnp.dot(
        slot_table.astype(jnp.float32),
        own_terms,
        precision=lax.Precision.HIGHEST,
        preferred_element_type=jnp.float32,
    )
    grad_terms = lax.all_to_all(
        term_slots.reshape(batch_count, capacity, embedding_dimension).astype(jnp.bfloat16),
        "batch",
        split_axis=0,
        concat_axis=0,
        tiled=True,
    ).astype(jnp.float32)
    spread = jnp.dot(
        return_table.astype(jnp.float32),
        grad_terms.reshape(slot_total, embedding_dimension),
        precision=lax.Precision.HIGHEST,
        preferred_element_type=jnp.float32,
    )
    passage_grad = norm_back(passages, pscale, unit_p + spread).astype(jnp.bfloat16)
    return (query_grad, passage_grad)


def local(queries, passages, hard_ids):
    pair_rows = queries.shape[0]
    query_grad, passage_grad, flags = exchange(hard_ids.reshape(1, pair_rows), queries, passages)
    return lax.cond(
        flags[0, 0] > 0,
        lambda: padded(queries, passages, hard_ids),
        lambda: (query_grad, passage_grad),
    )


def solution(mesh):
    in_specs = (P(("batch", "grp"), None), P(("batch", "grp"), None), P(("batch", "grp")))
    out_specs = (P(("batch", "grp"), None), P(("batch", "grp"), None))
    return jax.shard_map(local, mesh=mesh, in_specs=in_specs, out_specs=out_specs, check_vma=False)
```

```python
import functools

import jax
import jax.numpy as jnp
from jax import lax
from jax.experimental import pallas as pl
from jax.experimental.pallas import tpu as pltpu
from jax.sharding import PartitionSpec as P

SOFTMAX_TEMPER = 0.02
LOSS_SCALE = 64.0
EPSILON = 1e-06

PLANES = 16
PLANE = 8
FAR = PLANES // 2
SLOTS = 2
OWN = PLANE * SLOTS
CAPS = [0, 82, 74, 67, 58, 48, 37, 24, 8, 0]
LANES = 128
Q_AT = {1: (2,), 3: (3,), 5: (4,), 6: (5,), 7: (6,)}


def row_scales(values):
    floats = values.astype(jnp.float32)
    return lax.rsqrt(jnp.mean(floats * floats, -1, keepdims=True) + EPSILON)


def norm_back(values, scales, upstream):
    floats = values.astype(jnp.float32)
    return scales * upstream - scales * scales * scales * floats * jnp.mean(
        floats * upstream, -1, keepdims=True
    )


def offsets_of(sizes):
    out, total = [], 0
    for size in sizes:
        out.append(total)
        total += size
    return out, total


OUT_AT, OUT_ROWS = offsets_of([0] + [CAPS[d] for d in range(1, FAR + 1)])
CAP1 = CAPS[1]
SPLIT = 128


def parts_of(d):
    return [c for c in range(2) if CAPS[d] > c * SPLIT]


def part_of(d, c):
    return c * SPLIT, (CAPS[d] - SPLIT if c else min(CAPS[d], SPLIT))


def exchange_kernel(
    ids, queries, passages,
    query_grad, passage_grad, flags,
    q3, p3, qs, ps, qscale, pscale, column_ids, ids2, line_table, own_table, slot_table, asked,
    line_at, own_at, slot_at,
    gp, gq, out, final, qfirst, pstage, qstage, owed, floats, unit, scores, scores_t,
    ends, gathered, weights, sums,
    own_sem, x_send, x_recv, qz_send, qz_recv, pz_send, pz_recv,
    py_send, py_recv, qy_send, qy_recv, t_send, t_recv, c_send, c_recv, i_send, i_recv, table_sem, *arriving
):
    own = [[None, *arriving[(4 + s) * FAR : (5 + s) * FAR]] for s in range(2)]
    comb = [[None, *arriving[s * FAR : (s + 1) * FAR]] for s in range(2)]
    qin = [[None, *arriving[(2 + s) * FAR : (3 + s) * FAR]] for s in range(2)]
    rows, width = queries.shape
    lanes_per_row = width // LANES
    half = rows // 2
    b = lax.axis_index("batch")
    g = lax.axis_index("grp")
    n_grp = 4
    z, me = b // PLANE, b % PLANE

    def plane(step):
        return lax.rem(z + step + PLANES, PLANES)

    def peer(j):
        return lax.rem(me + j, PLANE)

    lines = [{"batch": plane(j) * PLANE + me} for j in range(1, PLANES)]
    ahead = [lines[0], lines[-1]]
    right, left = lax.rem(g + 1, n_grp), lax.rem(g + n_grp - 1, n_grp)
    sides = [{"grp": right}, {"grp": left}]
    peers = [{"batch": z * PLANE + peer(j)} for j in range(1, PLANE)]

    barrier = pltpu.get_barrier_semaphore()
    across = lax.rem(g + 2, n_grp)
    sides.append({"grp": across})
    greeted = lines + sides + peers
    for device in greeted:
        pl.semaphore_signal(barrier, inc=1, device_id=device, device_id_type=pl.DeviceIdType.MESH)

    def columns(i, size):
        return pl.ds(pl.multiple_of(i * size, size), size)

    def unit_rows(values, scales, short, spread):
        def square(i, total):
            part = values[:, columns(i, 256)].astype(jnp.float32)
            part = part * part
            return total + part[:, :LANES] + part[:, LANES:]

        total = lax.fori_loop(0, width // 256, square, jnp.zeros((rows, LANES), jnp.float32))
        scale_col = lax.rsqrt(jnp.sum(total, 1, keepdims=True) / width + EPSILON)
        scales[...] = scale_col
        for k in range(lanes_per_row):
            at = slice(k * LANES, (k + 1) * LANES)
            part = (values[:, at].astype(jnp.float32) * scale_col).astype(jnp.bfloat16)
            short[:, at] = part
            floats[pl.ds(k, rows, stride=lanes_per_row), :] = part.astype(jnp.float32)

        def narrow(r, carry):
            at = pl.ds(pl.multiple_of(r * lanes_per_row, lanes_per_row), lanes_per_row)
            spread[r] = floats[at, :].astype(jnp.bfloat16)
            return carry

        lax.fori_loop(0, rows, narrow, 0)

    sub = lax.broadcasted_iota(jnp.int32, (rows, LANES), 0)
    lane = lax.broadcasted_iota(jnp.int32, (rows, LANES), 1)

    def course_of(values, plane_of, me_of):
        oz, om = values >> 10, (values >> 7) & (PLANE - 1)
        ahead_of = (plane_of - oz) & (PLANES - 1)
        tie = (om + me_of) & 1
        side = jnp.where(ahead_of == 0, 2, jnp.where(ahead_of < FAR, 0, jnp.where(ahead_of == FAR, tie, 1)))
        return oz, om, side, jnp.where(ahead_of <= FAR, ahead_of, PLANES - ahead_of)

    def as_column(row):
        wide_row = jnp.broadcast_to(row.astype(jnp.float32), (rows, rows))
        return jnp.transpose(wide_row).astype(jnp.int32)

    def count_lanes(mask):
        return jnp.sum(jnp.where(mask, 1.0, 0.0), 1, keepdims=True).astype(jnp.int32)

    def pick_row(mask, values):
        return jnp.sum(jnp.where(mask, values.astype(jnp.float32), 0.0), 0, keepdims=True).astype(jnp.int32)

    def requests(row, plane_of):
        row = jnp.broadcast_to(row, (rows, LANES))
        col = as_column(row[0:1])
        _, _, side_r, dist_r = course_of(row, plane_of, me)
        oz, om, side, dist = course_of(col, plane_of, me)
        code_r = dist_r * LANES + (LANES - 1) - lane
        code = dist * LANES + (LANES - 1) - sub
        pos = count_lanes((side_r == side) & (code_r > code))
        slot = count_lanes(((row >> 7) == (col >> 7)) & (lane < sub))
        return oz, side, jnp.broadcast_to(pos, (rows, LANES)), om * SLOTS + jnp.minimum(slot, SLOTS - 1)

    unit_rows(queries, qscale, qs, q3)
    _, my_side, my_pos, my_cell = requests(ids[...], z)
    for s in range(2):
        own_table[s : s + 1, :] = jnp.minimum(pick_row((my_side == s) & (my_pos == lane), sub), rows - 1)
    home = jnp.where(my_side == 2, 2 * CAP1 + my_cell, my_side * CAP1 + jnp.minimum(my_pos, CAP1 - 1))
    own_table[2:3, :] = pick_row(sub == lane, home)
    own_copy = pltpu.make_async_copy(own_table, own_at, table_sem.at[0])
    own_copy.start()
    column_ids[b] = ids[...]
    pl.semaphore_wait(barrier, len(greeted))

    def remote(src, dst, send, recv, device):
        return pltpu.make_async_remote_copy(
            src_ref=src, dst_ref=dst, send_sem=send, recv_sem=recv,
            device_id=device, device_id_type=pl.DeviceIdType.MESH,
        )

    def settle(ref, sem):
        pltpu.make_async_copy(ref, ref, sem).wait()

    own_ids = column_ids.at[b]
    for device in peers:
        remote(own_ids, own_ids, i_send.at[0], i_recv.at[0], device).start()

    def block(ref, who, start=0, size=rows):
        return ref.at[pl.ds(pl.multiple_of(who * rows + start, half), size), :]

    whole = ((ps, gp), (qs, gq))
    locals_ = []

    def pass_on(a):
        dst = whole[a][1]
        for s, origin in ((0, left), (1, right)):
            remote(ps, block(dst, origin), x_send.at[a, s], x_recv.at[a, s], sides[s]).wait_recv()
            part = block(dst, origin, s * half, half)
            remote(part, part, x_send.at[a, 2 + s], x_recv.at[a, 2 + s], sides[s]).start()

    def x_end(a):
        dst = whole[a][1]
        for s in range(2):
            part = block(dst, across, s * half, half)
            remote(part, part, x_send.at[a, 2 + s], x_recv.at[a, 2 + s], sides[s]).wait()
            remote(ps, block(dst, g), x_send.at[a, s], x_recv.at[a, s], sides[s]).wait_send()

    def inside(at, count):
        return jnp.maximum(jnp.minimum(at, count - 1), 0)

    def copy_rows(n, store, load):
        def body(r, carry):
            store(r, load(r))
            return carry

        lax.fori_loop(0, n, body, 0, unroll=False)

    def q_hop(s, d, c):
        low, size = part_of(d, c)
        src = qfirst.at[s] if d == 1 else qin[s][d - 1]
        at = pl.ds(low, size)
        return remote(src.at[at], qin[s][d].at[at], qz_send.at[s, d, c], qz_recv.at[s, d, c], ahead[1 - s])

    own_copy.wait()
    for s in range(2):
        def store(r, value, s=s):
            qfirst[s, r] = value

        def load(r, s=s):
            return q3[inside(own_at[s, r], rows)]

        copy_rows(CAP1, store, load)
        for c in parts_of(1):
            q_hop(s, 1, c).start()

    settle(column_ids.at[pl.ds(0, PLANE - 1)], i_recv.at[0])
    plane_ids = column_ids.at[pl.ds(z * PLANE, PLANE)]
    for device in lines:
        remote(plane_ids, plane_ids, i_send.at[1], i_recv.at[1], device).start()
    unit_rows(passages, pscale, ps, p3)

    for a, (src, dst) in enumerate(whole):
        copy = pltpu.make_async_copy(src, block(dst, g), own_sem.at[a])
        copy.start()
        locals_.append(copy)
        for s in range(2):
            remote(src, block(dst, g), x_send.at[a, s], x_recv.at[a, s], sides[s]).start()

    settle(column_ids.at[pl.ds(0, PLANE * (PLANES - 1))], i_recv.at[1])

    def flat(r, carry):
        ids2[pl.ds(r, 1), :] = column_ids[r]
        return carry

    lax.fori_loop(0, PLANES * PLANE, flat, 0)

    wanted = (ids2[...] >> 7) == b
    code = (lane * LANES + (ids2[...] & (LANES - 1))).astype(jnp.float32)
    asks = count_lanes(wanted)
    first = jnp.min(jnp.where(wanted, code, float(LANES * LANES)), 1, keepdims=True).astype(jnp.int32)
    last = jnp.max(jnp.where(wanted, code, 0.0), 1, keepdims=True).astype(jnp.int32)
    first = jnp.where(asks > 0, first, 0)
    askers = [jnp.where(asks > 0, first >> 7, -1), jnp.where(asks > 1, last >> 7, -1)]
    offsets = [first & (LANES - 1), last & (LANES - 1)]
    slot_table[...] = jnp.where(lane == 0, offsets[0], offsets[1])
    slot_copy = pltpu.make_async_copy(slot_table, slot_at, table_sem.at[1])
    slot_copy.start()
    asked[...] = jnp.where(
        lane == 0, askers[0], jnp.where(lane == 1, offsets[0], jnp.where(lane == 2, askers[1], offsets[1]))
    )

    def line_rows(source, carry):
        oz, side, pos, cell = requests(ids2[pl.ds(source * PLANE + me, 1), :], source)
        here = oz == z
        for s in range(2):
            hit = here & (side == s) & (pos == lane)
            placed = jnp.minimum(pick_row(hit, cell + 1) - 1, OWN - 1)
            far = lax.rem((source - z if s == 0 else z - source) + PLANES, PLANES)
            room = 0
            for d in range(1, FAR):
                room = jnp.where(far == d, CAPS[d + 1], room)
            filler = SLOTS * peer(s)
            other = jnp.where(lane[0:1] < room, OWN, filler)
            line_table[pl.ds(s * PLANES + source, 1), :] = jnp.where(placed >= 0, placed, other)
        place = jnp.where(side == 2, sub, pos)
        far = lax.rem(source - z + PLANES, PLANES)
        limit = rows - 1
        for d in range(1, FAR + 1):
            limit = jnp.where((far == d) | (far == PLANES - d), CAPS[d] - 1, limit)
        line_table[pl.ds(2 * PLANES + source, 1), :] = jnp.minimum(pick_row(here & (cell == lane), place), limit)
        return carry

    lax.fori_loop(0, PLANES, line_rows, 0)
    line_copy = pltpu.make_async_copy(line_table, line_at, table_sem.at[2])
    line_copy.start()
    slot_copy.wait()
    line_copy.wait()

    def p_owed(s, d):
        return plane(d) if s == 0 else plane(-d)

    def partners(s, d):
        return range(s, PLANE, 2) if d == FAR else range(PLANE)

    def p_spread(s, d):
        target = p_owed(s, d)
        place = pl.ds(me * SLOTS, SLOTS)
        others = 0
        for j in partners(s, d):
            for k in range(SLOTS):
                row = p3[inside(slot_at[target * PLANE + peer(j), k], rows)]
                if j == 0:
                    own[s][d][me * SLOTS + k] = row
                else:
                    pstage[s, d, others * SLOTS + k] = row
            if j:
                others += 1
        others = 0
        for j in partners(s, d):
            if j:
                remote(
                    pstage.at[s, d, pl.ds(others * SLOTS, SLOTS)], own[s][d].at[place],
                    py_send.at[s, d], py_recv.at[s, d], peers[j - 1],
                ).start()
                others += 1

    def p_spread_near():
        near = 2 * CAP1
        for k in range(SLOTS):
            final[near + me * SLOTS + k] = p3[inside(slot_at[z * PLANE + me, k], rows)]
        for j in range(1, PLANE):
            for k in range(SLOTS):
                pstage[0, 0, (j - 1) * SLOTS + k] = p3[inside(slot_at[z * PLANE + peer(j), k], rows)]
        for j in range(1, PLANE):
            remote(
                pstage.at[0, 0, pl.ds((j - 1) * SLOTS, SLOTS)],
                final.at[pl.ds(near + me * SLOTS, SLOTS)],
                py_send.at[0, 0], py_recv.at[0, 0], peers[j - 1],
            ).start()

    def spread_bytes(s, d):
        n = SLOTS * len([j for j in partners(s, d) if j])
        return pstage.at[s, d, pl.ds(0, n)]

    for d in range(FAR, 0, -1):
        for s in range(2):
            p_spread(s, d)
    p_spread_near()

    def p_hop(s, d, c):
        low, size = part_of(d, c)
        src = out.at[s, pl.ds(OUT_AT[d] + low, size)]
        dst = final.at[pl.ds(s * CAP1 + low, size)] if d == 1 else comb[s][d - 1].at[pl.ds(low, size)]
        return remote(src, dst, pz_send.at[s, d, c], pz_recv.at[s, d, c], ahead[s])

    def p_step(s, d, c):
        if c == 0:
            settle(spread_bytes(s, d), py_recv.at[s, d])
        low, size = part_of(d, c)
        target = p_owed(s, d)
        passing = 0
        if c in parts_of(d + 1):
            p_hop(s, d + 1, c).wait_recv()
            passing = part_of(d + 1, c)[1]

        def cell(r):
            return line_at[s * PLANES + target, r]

        def store(r, value):
            out[s, OUT_AT[d] + low + r] = value

        def load(r):
            at = cell(low + r)
            here = own[s][d][inside(at, OWN)]
            return lax.select(at < OWN, here, comb[s][d][low + r])

        copy_rows(passing, store, load)

        def store_new(r, value):
            out[s, OUT_AT[d] + low + passing + r] = value

        def load_new(r):
            return own[s][d][inside(cell(low + passing + r), OWN)]

        copy_rows(size - passing, store_new, load_new)
        p_hop(s, d, c).start()

    def q_spread(s, d):
        source = plane(d) if s == 0 else plane(-d)

        def take(j, k):
            at = line_at[2 * PLANES + source, peer(j) * SLOTS + k]
            if d == 0:
                return q3[inside(at, rows)]
            return qin[j % 2 if d == FAR else s][d][inside(at, CAPS[d])]

        place = owed.at[:, source, me]
        line = 2 * d + s
        for j in range(PLANE):
            for k in range(SLOTS):
                qstage[line, j * SLOTS + k] = take(j, k)
        pltpu.make_async_copy(
            qstage.at[line, pl.ds(0, SLOTS)], place, own_sem.at[2 + line]
        ).start()
        for j in range(1, PLANE):
            remote(
                qstage.at[line, pl.ds(j * SLOTS, SLOTS)], place,
                qy_send.at[line], qy_recv.at[line], peers[j - 1],
            ).start()

    def q_step(d):
        for c in parts_of(d):
            for s in range(2):
                q_hop(s, d, c).wait_recv()
                if c in parts_of(d + 1):
                    q_hop(s, d + 1, c).start()
        for s in range(2):
            if d < FAR or s == 0:
                q_spread(s, d)

    scale = 1.0 / (width * SOFTMAX_TEMPER)
    factor = LOSS_SCALE * scale

    def score(dst, a, others):
        dst[...] = jnp.zeros_like(dst)
        chunk = 512

        def body(i, carry):
            at = columns(i, chunk)
            dst[...] += lax.dot_general(
                a[:, at], others[:, at], (((1,), (1,)), ((), ())), preferred_element_type=jnp.float32
            )
            return carry

        lax.fori_loop(0, width // chunk, body, 0)
        dst[...] = dst[...] * scale

    def laid_out(k, n):
        return floats[pl.ds(k, n, stride=lanes_per_row), :]

    def as_row(column_values):
        return jnp.transpose(jnp.broadcast_to(column_values, (rows, rows)))[0:1, :]

    def finish(values, scales, dots, result):
        scale_col = scales[...]
        weight = scale_col * scale_col * scale_col * (jnp.sum(dots, 1, keepdims=True) / width)

        def body(i, carry):
            at = columns(i, 256)
            result[:, at] = (
                scale_col * unit[:, at] - weight * values[:, at].astype(jnp.float32)
            ).astype(jnp.bfloat16)
            return carry

        lax.fori_loop(0, width // 256, body, 0)

    def product(weight_rows, group):
        def body(i, carry):
            at = columns(i, 256)
            unit[:, at] = jnp.dot(weight_rows, group[:, at], preferred_element_type=jnp.float32)
            return carry

        lax.fori_loop(0, width // 256, body, 0)

    q_spread(0, 0)
    q_step(1)
    for step in range(1, FAR + 1):
        for c in parts_of(FAR + 1 - step):
            for s in range(2):
                p_step(s, FAR + 1 - step, c)
        for d in Q_AT.get(step, ()):
            q_step(d)
        if step == 2:
            pass_on(0)
        if step == 3:
            pass_on(1)
        if step == 5:
            x_end(0)
            for copy in locals_:
                copy.wait()
            score(scores, qs, gp)
            sums[...] = jnp.sum(jnp.exp(scores[...]), 1, keepdims=True)
        if step == 4:
            who = (sub >> 3, sub & (PLANE - 1))
            _, _, side, dist = course_of(ids2[...], *who)
            over = jnp.zeros((rows, 1), jnp.float32)
            for s in range(2):
                for d in range(1, FAR):
                    over = jnp.maximum(over, jnp.where(count_lanes((side == s) & (dist >= d)) > CAPS[d], 1.0, 0.0))
            flag = jnp.max(jnp.broadcast_to(over, (rows, LANES)), 0, keepdims=True)
        if step == 6:
            x_end(1)
            score(scores_t, ps, gq)

    for s in range(2):
        for c in parts_of(1):
            p_hop(s, 1, c).wait_recv()
    here = spread_bytes(0, 0)
    pltpu.make_async_copy(here, here, py_recv.at[0, 0]).wait()

    def store(r, value):
        floats[pl.ds(pl.multiple_of(r * lanes_per_row, lanes_per_row), lanes_per_row), :] = value.astype(
            jnp.float32
        )

    def load(r):
        return final[inside(own_at[2, r], 2 * CAP1 + OWN)]

    copy_rows(rows, store, load)

    dots = jnp.zeros((rows, LANES), jnp.float32)
    for k in range(lanes_per_row):
        dots += laid_out(k, rows) * qs[:, k * LANES : (k + 1) * LANES].astype(jnp.float32)
    hard_score = jnp.sum(dots, 1, keepdims=True) * scale
    totals = jnp.log(sums[...] + jnp.exp(hard_score))
    hard_w = jnp.exp(hard_score - totals).astype(jnp.bfloat16).astype(jnp.float32)

    ends[g, 0] = as_row(totals)
    ends[g, 1] = flag
    weights[me, z] = as_row(hard_w)
    t_copies = [remote(ends.at[g], ends.at[g], t_send.at[i], t_recv.at[i], sides[i]) for i in range(3)]
    for copy in t_copies:
        copy.start()
    own_row = weights.at[me, z]
    for device in lines:
        remote(own_row, own_row, c_send.at[0], c_recv.at[0], device).start()

    q_step(FAR - 1)

    row_at = lax.broadcasted_iota(jnp.int32, scores.shape, 0)
    col_at = lax.broadcasted_iota(jnp.int32, scores.shape, 1)
    positive = jnp.where(col_at == row_at + g * rows, 1.0, 0.0)
    product((jnp.exp(scores[...] - totals) - positive).astype(jnp.bfloat16), gp)
    dots = jnp.zeros((rows, LANES), jnp.float32)
    for k in range(lanes_per_row):
        at = slice(k * LANES, (k + 1) * LANES)
        value = (unit[:, at] + hard_w * laid_out(k, rows)) * factor
        unit[:, at] = value
        dots += queries[:, at].astype(jnp.float32) * value
    finish(queries, qscale, dots, query_grad)

    settle(weights.at[0, pl.ds(0, PLANES - 1)], c_recv.at[0])
    own_line = weights.at[me]
    for device in peers:
        remote(own_line, own_line, c_send.at[1], c_recv.at[1], device).start()
    q_step(FAR)

    for copy in t_copies:
        copy.wait()
    group_totals = jnp.concatenate([ends[i, 0] for i in range(n_grp)], axis=1)
    flags[...] = jnp.maximum(jnp.maximum(ends[0, 1], ends[1, 1]), jnp.maximum(ends[2, 1], ends[3, 1]))
    product((jnp.exp(scores_t[...] - group_totals) - positive).astype(jnp.bfloat16), gq)

    settle(weights.at[pl.ds(0, PLANE - 1)], c_recv.at[1])
    for who in range(PLANE):
        for at in range(PLANES):
            gathered[pl.ds(at * PLANE + who, 1), :] = weights[who, at]
    placed = []
    for k in range(SLOTS):
        asker, offset = asked[:, 2 * k : 2 * k + 1], asked[:, 2 * k + 1 : 2 * k + 2]
        slot_w = jnp.sum(jnp.where(lane == asker, gathered[...], 0.0), 1, keepdims=True)
        placed.append(jnp.transpose(jnp.where(lane == offset, slot_w, 0.0)))
    spread_w = jnp.concatenate(placed, axis=1).astype(jnp.bfloat16)

    for d in range(FAR + 1):
        for s in range(2):
            if (d == 0 or d == FAR) and s == 1:
                continue
            line = 2 * d + s
            sent = qstage.at[line, pl.ds(SLOTS, OWN - SLOTS)]
            settle(sent, qy_recv.at[line])
            settle(qstage.at[line, pl.ds(0, SLOTS)], own_sem.at[2 + line])

    for k in range(SLOTS):
        for who in range(PLANE):

            def widen(r, carry, k=k, who=who):
                at = pl.multiple_of(((k * PLANES + r) * PLANE + who) * lanes_per_row, lanes_per_row)
                floats[pl.ds(at, lanes_per_row), :] = owed[k, r, who].astype(jnp.float32)
                return carry

            lax.fori_loop(0, PLANES, widen, 0)
    dots = jnp.zeros((rows, LANES), jnp.float32)
    for k in range(0, lanes_per_row, 2):
        at = slice(k * LANES, (k + 2) * LANES)
        pair = jnp.concatenate([laid_out(k, SLOTS * rows), laid_out(k + 1, SLOTS * rows)], axis=1)
        value = unit[:, at] + jnp.dot(spread_w, pair.astype(jnp.bfloat16), preferred_element_type=jnp.float32)
        value = value * factor
        unit[:, at] = value
        both = passages[:, at].astype(jnp.float32) * value
        dots += both[:, :LANES] + both[:, LANES:]
    finish(passages, pscale, dots, passage_grad)

    settle(column_ids.at[pl.ds(0, PLANE - 1)], i_send.at[0])
    settle(column_ids.at[pl.ds(0, PLANE * (PLANES - 1))], i_send.at[1])
    settle(weights.at[0, pl.ds(0, PLANES - 1)], c_send.at[0])
    settle(weights.at[pl.ds(0, PLANE - 1)], c_send.at[1])
    for d in range(FAR + 1):
        for s in range(2):
            if (d == 0 or d == FAR) and s == 1:
                continue
            line = 2 * d + s
            settle(qstage.at[line, pl.ds(SLOTS, OWN - SLOTS)], qy_send.at[line])
    for d in range(FAR + 1):
        for s in range(2):
            if d == 0 and s == 1:
                continue
            here = spread_bytes(s, d)
            pltpu.make_async_copy(here, here, py_send.at[s, d]).wait()
            if d > 0:
                for c in parts_of(d):
                    q_hop(s, d, c).wait_send()
                    p_hop(s, d, c).wait_send()


def exchange(ids, queries, passages):
    rows, width = queries.shape
    line = (width // LANES, LANES)
    vmem = pl.BlockSpec(memory_space=pltpu.VMEM)
    dma = pltpu.SemaphoreType.DMA

    def buffer(*lead):
        return pltpu.VMEM(lead + line, jnp.bfloat16)

    def wide(*shape):
        return pltpu.VMEM(shape, jnp.float32)

    def table(*shape):
        return pltpu.VMEM(shape, jnp.int32)

    return pl.pallas_call(
        exchange_kernel,
        out_shape=(
            jax.ShapeDtypeStruct((rows, width), jnp.bfloat16),
            jax.ShapeDtypeStruct((rows, width), jnp.bfloat16),
            jax.ShapeDtypeStruct((1, LANES), jnp.float32),
        ),
        in_specs=[vmem] * 3,
        out_specs=(vmem, vmem, vmem),
        scratch_shapes=[
            buffer(rows),
            buffer(rows),
            pltpu.VMEM((rows, width), jnp.bfloat16),
            pltpu.VMEM((rows, width), jnp.bfloat16),
            wide(rows, 1),
            wide(rows, 1),
            table(PLANES * PLANE, 1, LANES),
            table(PLANES * PLANE, LANES),
            table(3 * PLANES, LANES),
            table(8, LANES),
            table(PLANES * PLANE, LANES),
            table(PLANES * PLANE, LANES),
            pltpu.SMEM((3 * PLANES, LANES), jnp.int32),
            pltpu.SMEM((8, LANES), jnp.int32),
            pltpu.SMEM((PLANES * PLANE, LANES), jnp.int32),
            pltpu.VMEM((4 * rows, width), jnp.bfloat16),
            pltpu.VMEM((4 * rows, width), jnp.bfloat16),
            buffer(2, OUT_ROWS),
            buffer(2 * CAP1 + OWN),
            buffer(2, CAP1),
            buffer(2, FAR + 1, OWN),
            buffer(2 * (FAR + 1), OWN),
            buffer(SLOTS, PLANES, PLANE),
            wide(SLOTS * rows * line[0], LANES),
            wide(rows, width),
            wide(rows, 4 * rows),
            wide(rows, 4 * rows),
            wide(4, 2, 1, LANES),
            wide(PLANE * PLANES, LANES),
            wide(PLANE, PLANES, 1, LANES),
            wide(rows, 1),
            dma((2 + 2 * (FAR + 1),)),
            dma((2, 4)), dma((2, 4)),
            dma((2, FAR + 1, 2)), dma((2, FAR + 1, 2)),
            dma((2, FAR + 1, 2)), dma((2, FAR + 1, 2)),
            dma((2, FAR + 1)), dma((2, FAR + 1)),
            dma((2 * (FAR + 1),)), dma((2 * (FAR + 1),)),
            dma((3,)), dma((3,)),
            dma((2,)), dma((2,)),
            dma((2,)), dma((2,)), dma((3,)),
            *[buffer(max(CAPS[d + 1], OWN)) for _ in range(2) for d in range(1, FAR + 1)],
            *[buffer(CAPS[d]) for _ in range(2) for d in range(1, FAR + 1)],
            *[buffer(OWN) for _ in range(2 * FAR)],
        ],
        compiler_params=pltpu.CompilerParams(
            collective_id=0, has_side_effects=True, vmem_limit_bytes=62 * 1024 * 1024
        ),
        cost_estimate=pl.CostEstimate(
            flops=2 * 2 * 2 * rows * 4 * rows * width, bytes_accessed=8 * 1024 * 1024, transcendentals=0
        ),
        name="exchange",
    )(ids, queries, passages)


def padded(queries, passages, hard_ids):
    pair_rows, embedding_dimension = queries.shape
    batch_count = lax.axis_size("batch")
    group_number_total = lax.axis_size("grp")
    group_pos = lax.axis_index("grp")
    capacity = 2 * ((pair_rows + batch_count - 1) // batch_count)
    slot_total = batch_count * capacity
    group_rows = group_number_total * pair_rows
    inverse_permutation = 1.0 / (embedding_dimension * SOFTMAX_TEMPER)
    factor = LOSS_SCALE * inverse_permutation
    qscale = row_scales(queries)
    pscale = row_scales(passages)
    qshort = (queries.astype(jnp.float32) * qscale).astype(jnp.bfloat16)
    pshort = (passages.astype(jnp.float32) * pscale).astype(jnp.bfloat16)
    owners = hard_ids // pair_rows
    offsets = hard_ids % pair_rows
    local_rows = jnp.arange(pair_rows)
    same_owner = owners[:, None] == owners[None, :]
    earlier = local_rows[:, None] > local_rows[None, :]
    rank_in = jnp.sum((same_owner & earlier).astype(jnp.int32), 1)
    slot_index = owners * capacity + rank_in
    slot_table = jnp.arange(slot_total)[:, None] == slot_index[None, :]
    requests = jnp.sum(jnp.where(slot_table, offsets[None, :], 0), 1)
    requests = requests.reshape(batch_count, capacity)
    served_req = lax.all_to_all(requests, "batch", split_axis=0, concat_axis=0, tiled=True)
    served_flat = served_req.reshape(-1)
    served = jnp.take(pshort, served_flat, axis=0).reshape(
        batch_count, capacity, embedding_dimension
    )
    arrived = lax.all_to_all(served, "batch", split_axis=0, concat_axis=0, tiled=True)
    hard_p = jnp.take(arrived.reshape(slot_total, embedding_dimension), slot_index, axis=0)
    group_p, group_q = (
        lax.all_gather(pshort, "grp", axis=0, tiled=True),
        lax.all_gather(qshort, "grp", axis=0, tiled=True),
    )
    own_cols = group_pos * pair_rows + local_rows
    positive = (jnp.arange(group_rows)[None, :] == own_cols[:, None]).astype(jnp.float32)
    inner_scores = (
        jnp.dot(qshort, group_p.T, preferred_element_type=jnp.float32) * inverse_permutation
    )
    hard_score = (
        jnp.einsum("rd,rd->r", qshort, hard_p, preferred_element_type=jnp.float32)
        * inverse_permutation
    )
    totals = jnp.log(jnp.sum(jnp.exp(inner_scores), 1) + jnp.exp(hard_score))
    inner_w = (jnp.exp(inner_scores - totals[:, None]) - positive).astype(jnp.bfloat16)
    hard_w = jnp.exp(hard_score - totals).astype(jnp.bfloat16)
    unit_q = (
        jnp.dot(inner_w, group_p, preferred_element_type=jnp.float32)
        + hard_w.astype(jnp.float32)[:, None] * hard_p
    ) * factor
    query_grad = norm_back(queries, qscale, unit_q).astype(jnp.bfloat16)
    group_totals = lax.all_gather(totals, "grp", axis=0, tiled=True)
    scores = jnp.dot(group_q, pshort.T, preferred_element_type=jnp.float32) * inverse_permutation
    weight_factors = (jnp.exp(scores - group_totals[:, None]) - positive.T).astype(jnp.bfloat16)
    unit_p = jnp.dot(weight_factors.T, group_q, preferred_element_type=jnp.float32) * factor
    return_table = local_rows[:, None] == served_flat[None, :]
    own_terms = hard_w.astype(jnp.float32)[:, None] * qshort * factor
    term_slots = jnp.dot(
        slot_table.astype(jnp.float32),
        own_terms,
        precision=lax.Precision.HIGHEST,
        preferred_element_type=jnp.float32,
    )
    grad_terms = lax.all_to_all(
        term_slots.reshape(batch_count, capacity, embedding_dimension).astype(jnp.bfloat16),
        "batch",
        split_axis=0,
        concat_axis=0,
        tiled=True,
    ).astype(jnp.float32)
    spread = jnp.dot(
        return_table.astype(jnp.float32),
        grad_terms.reshape(slot_total, embedding_dimension),
        precision=lax.Precision.HIGHEST,
        preferred_element_type=jnp.float32,
    )
    passage_grad = norm_back(passages, pscale, unit_p + spread).astype(jnp.bfloat16)
    return (query_grad, passage_grad)


def local(queries, passages, hard_ids):
    pair_rows = queries.shape[0]
    query_grad, passage_grad, flags = exchange(hard_ids.reshape(1, pair_rows), queries, passages)
    return lax.cond(
        flags[0, 0] > 0,
        lambda: padded(queries, passages, hard_ids),
        lambda: (query_grad, passage_grad),
    )


def solution(mesh):
    in_specs = (P(("batch", "grp"), None), P(("batch", "grp"), None), P(("batch", "grp")))
    out_specs = (P(("batch", "grp"), None), P(("batch", "grp"), None))
    return jax.shard_map(local, mesh=mesh, in_specs=in_specs, out_specs=out_specs, check_vma=False)
```
